256 devices in a mesh: section: 4 (over z_lo, core), seq: 4 (over y), head: 16 (over x, z_hi).
Axes of the slice: x: 4, y: 4, z: 8 (z_hi: 4, z_lo: 2; z = z_hi * 2 + z_lo), core: 2. Of those that a mesh axis runs over, the one named last changes fastest.
Arguments:
- hidden: bfloat16 [4, 2048, 4608], P(None, ('section', 'seq'), 'head')
- critique: bfloat16 [4, 4, 4608], P('seq', None, 'head')
- lengths: int32 [4], replicated, may hold values from 512 to 2048, as said below
- pre_gain: bfloat16 [4608], replicated, may hold values from 0.099609375 to 1.8984375
- post_gain: bfloat16 [4608], P('head'), may hold values from 0.099609375 to 1.8984375
- q_weight: bfloat16 [4608, 4096], P(None, 'head'), may hold values from -0.09375 to 0.09375
- k_weight: bfloat16 [4608, 2048], P(None, 'head'), may hold values from -0.09375 to 0.09375
- v_weight: bfloat16 [4608, 2048], P(None, 'head')
- o_weight: bfloat16 [4096, 4608], P('head')
Outputs:
- hidden_out: bfloat16 [4, 2048, 4608], P(None, ('section', 'seq'), 'head')
- critique_out: bfloat16 [4, 4, 4608], P('seq', None, 'head')
The draws below stay inside these ranges and needn't reach their ends.
Inputs may be any that keep to these rules, and one draw needn't show every extreme that they name: `lengths`: one pair fills all 2048 slots and one uses 2048/4 of them.
All inputs are finite; a program needn't handle non-finite values.
Results may differ from the reference program's by a relative error of at most 0.007.
Values may be sent and summed in bfloat16 or wider, within the bound.
A program may use at most 128 MiB of HBM per device.

```python
import math
import jax
import jax.numpy as jnp
from jax import lax

D = 4608
HEADS = 32
KV_HEADS = 16
HEAD = 128
ROWS = 4
LEN = 2048
STEPS = 4


def rescale(key, base_draw):
    row_key, column_key = jax.random.split(key, 2)
    row_scale = jnp.exp(jax.random.uniform(row_key, base_draw.shape[:-1] + (1,), jnp.float32, -1.15, 1.15))
    column_scale = jnp.exp(jax.random.uniform(column_key, base_draw.shape[-1:], jnp.float32, -1.15, 1.15))
    return base_draw * row_scale * column_scale


def blend_heads(own_part, common_part, share):
    return math.sqrt(1.0 - share) * own_part + math.sqrt(share) * common_part


def draw_hidden(key, part):
    key = jax.random.fold_in(key, 3)
    front_key, scale_key = jax.random.split(key)
    full_shape = (ROWS, LEN, D)
    base_draw = jax.random.normal(front_key, full_shape, jnp.float32)
    return rescale(scale_key, base_draw).astype(jnp.bfloat16)


def draw_critique(key, part):
    key = jax.random.fold_in(key, 5)
    front_key, scale_key = jax.random.split(key)
    full_shape = (ROWS, STEPS, D)
    base_draw = jax.random.normal(front_key, full_shape, jnp.float32)
    return rescale(scale_key, base_draw).astype(jnp.bfloat16)


def draw_lengths(key, part):
    key = jax.random.fold_in(key, 11)
    front_key, order_key = jax.random.split(key)
    drawn = jax.random.randint(front_key, (ROWS,), LEN // 4, LEN + 1)
    picked = jax.random.permutation(order_key, ROWS)
    drawn = drawn.at[picked[0]].set(LEN)
    drawn = drawn.at[picked[1]].set(LEN // 4)
    return drawn.astype(jnp.int32)


def draw_v_weight(key, part):
    key = jax.random.fold_in(key, 17)
    own_key, common_key = jax.random.split(key)
    common_part = jax.random.normal(common_key, (D, 1, HEAD), jnp.float32)
    own_part = jax.random.normal(own_key, (D, KV_HEADS, HEAD), jnp.float32)
    mixed = blend_heads(own_part, common_part, 0.4)
    return (mixed.reshape(D, KV_HEADS * HEAD) * D ** (-0.5)).astype(jnp.bfloat16)


def draw_o_weight(key, part):
    key = jax.random.fold_in(key, 23)
    own_key, common_key = jax.random.split(key)
    common_part = jax.random.normal(common_key, (1, HEAD, D), jnp.float32)
    own_part = jax.random.normal(own_key, (HEADS, HEAD, D), jnp.float32)
    mixed = blend_heads(own_part, common_part, 0.4)
    return (mixed.reshape(HEADS * HEAD, D) * (HEADS * HEAD) ** (-0.5)).astype(jnp.bfloat16)


def level_of(key, extent, pieces, low, largest):
    def one(dim, blocks):
        heights = jax.random.uniform(jax.random.fold_in(jax.random.fold_in(key, 6), dim), (blocks,), jnp.float32, low / len(pieces), largest / len(pieces))
        return jnp.repeat(jnp.exp(heights), extent[dim] // blocks).reshape((-1,) + (1,) * (len(extent) - dim - 1))

    level = one(*pieces[0])
    for cut in pieces[1:]:
        level = level * one(*cut)
    return level


def gaussian(stream_key, dims, spread, limit, pieces=(), kind=jnp.bfloat16):
    values = spread * jax.random.normal(stream_key, dims, jnp.float32)
    if pieces:
        values = values * level_of(stream_key, dims, pieces, -0.22, 0.18)
    return jnp.clip(values, -limit, limit).astype(kind)


def setup_inputs(seed: int = 0) -> dict:
    key_list = jax.random.split(jax.random.key(seed), 10)
    return {
        "hidden": draw_hidden(jax.random.fold_in(key_list[9], 71), 0),
        "critique": draw_critique(jax.random.fold_in(key_list[9], 71), 0),
        "lengths": draw_lengths(jax.random.fold_in(key_list[9], 71), 0),
        "pre_gain": jnp.clip(1.0 + 0.18 * jax.random.normal(key_list[3], (D,), jnp.float32), 0.099609375, 1.8984375).astype(jnp.bfloat16),
        "post_gain": jnp.clip(1.0 + 0.18 * jax.random.normal(key_list[4], (D,), jnp.float32), 0.099609375, 1.8984375).astype(jnp.bfloat16),
        "q_weight": gaussian(key_list[5], (D, HEADS * HEAD), D ** -0.5, 0.09375, ((1, 16),)),
        "k_weight": gaussian(key_list[6], (D, KV_HEADS * HEAD), D ** -0.5, 0.09375, ((1, 16),)),
        "v_weight": draw_v_weight(jax.random.fold_in(key_list[9], 71), 0),
        "o_weight": draw_o_weight(jax.random.fold_in(key_list[9], 71), 0),
    }


epsilon = 1e-06
soft_cap = 50.0
rope_base = 10000.0

def norm_scale(inputs, gain_vector):
    floats = inputs.astype(jnp.float32)
    mean_square = lax.optimization_barrier(jnp.mean(floats * floats, axis=-1, keepdims=True))
    return (floats * lax.rsqrt(mean_square + epsilon) * gain_vector.astype(jnp.float32)).astype(jnp.bfloat16)

def rotate(inputs, positions):
    half_size = inputs.shape[-1] // 2
    frequency = jnp.exp(jnp.arange(half_size, dtype=jnp.float32) * (-2.0 * math.log(rope_base) / inputs.shape[-1]))
    rotation = positions[..., None, None] * frequency
    cosine = jnp.cos(rotation)
    sine_part = jnp.sin(rotation)
    front_half = inputs[..., :half_size]
    second = inputs[..., half_size:]
    return jnp.concatenate([front_half * cosine - second * sine_part, second * cosine + front_half * sine_part], axis=-1)

def heads_of(inputs, positions, pre_gain, q_weight, k_weight, v_weight):
    batch_rows = inputs.shape[0]
    span_here = inputs.shape[1]
    normed = norm_scale(inputs, pre_gain).reshape(batch_rows * span_here, D)
    queries = jnp.dot(normed, q_weight, preferred_element_type=jnp.float32).reshape(batch_rows, span_here, HEADS, HEAD)
    queries = rotate(queries, positions).astype(jnp.bfloat16).reshape(batch_rows, span_here, KV_HEADS, HEADS // KV_HEADS, HEAD)
    key_rows = jnp.dot(normed, k_weight, preferred_element_type=jnp.float32).reshape(batch_rows, span_here, KV_HEADS, HEAD)
    key_rows = rotate(key_rows, positions).astype(jnp.bfloat16)
    value_rows = jnp.dot(normed, v_weight, preferred_element_type=jnp.float32).astype(jnp.bfloat16)
    return (queries, key_rows, value_rows.reshape(batch_rows, span_here, KV_HEADS, HEAD))

def attend(query_rows, key_rows, value_rows, key_mask, score_scale):
    scores = jnp.einsum('tjd,kd->tjk', query_rows.astype(jnp.float32), key_rows.astype(jnp.float32)) * score_scale
    scores = soft_cap * jnp.tanh(scores / soft_cap)
    weight = jnp.where(key_mask[:, None, :], jnp.exp(scores), 0.0)
    weight_total = lax.optimization_barrier(jnp.sum(weight, axis=-1))
    rounded = lax.optimization_barrier(weight.astype(jnp.bfloat16))
    summed = jnp.einsum('tjk,kd->tjd', rounded.astype(jnp.float32), value_rows.astype(jnp.float32))
    return (summed / weight_total[..., None]).astype(jnp.bfloat16)

def by_head(array):
    moved = jnp.moveaxis(array, 2, 1)
    return moved.reshape((moved.shape[0] * moved.shape[1],) + moved.shape[2:])

def finish(residual, attended, post_gain, o_weight):
    projected = jnp.dot(attended, o_weight, preferred_element_type=jnp.float32)
    mean_square = lax.optimization_barrier(jnp.mean(projected * projected, axis=-1, keepdims=True))
    flat_rows = residual.reshape(-1, D).astype(jnp.float32)
    result = flat_rows + projected * lax.rsqrt(mean_square + epsilon) * post_gain.astype(jnp.float32)
    return result.astype(jnp.bfloat16).reshape(residual.shape)

def reference(hidden, critique, lengths, pre_gain, post_gain, q_weight, k_weight, v_weight, o_weight):
    group_size = HEADS // KV_HEADS
    score_scale = (D // HEADS) ** (-0.5)
    positions = jnp.broadcast_to(jnp.arange(LEN, dtype=jnp.float32)[None, :], (ROWS, LEN))
    queries, key_rows, value_rows = heads_of(hidden, positions, pre_gain, q_weight, k_weight, v_weight)
    head_lengths = jnp.repeat(lengths, KV_HEADS)
    position_index = jnp.arange(LEN, dtype=jnp.int32)

    def prefill_one(work_item):
        query_rows, key_part, value_part, row_length = work_item
        key_mask = (position_index[None, :] <= position_index[:, None]) & (position_index[None, :] < row_length)
        return attend(query_rows, key_part, value_part, key_mask, score_scale)
    attended = lax.map(prefill_one, (by_head(queries), by_head(key_rows), by_head(value_rows), head_lengths))
    attended = jnp.moveaxis(attended.reshape(ROWS, KV_HEADS, LEN, group_size, HEAD), 1, 2).reshape(ROWS * LEN, HEADS * HEAD)
    hidden_out = finish(hidden, attended, post_gain, o_weight)
    step_positions = (lengths[:, None] + jnp.arange(STEPS, dtype=jnp.int32)[None, :]).astype(jnp.float32)
    new_queries, new_keys, new_values = heads_of(critique, step_positions, pre_gain, q_weight, k_weight, v_weight)
    joined_keys = jnp.concatenate([key_rows, new_keys], axis=1)
    joined_values = jnp.concatenate([value_rows, new_values], axis=1)
    step_order = jnp.arange(STEPS, dtype=jnp.int32)

    def critique_one(work_item):
        query_rows, key_part, value_part, row_length = work_item
        cached = jnp.broadcast_to((position_index < row_length)[None, :], (STEPS, LEN))
        own_part = step_order[None, :] <= step_order[:, None]
        key_mask = jnp.concatenate([cached, own_part], axis=1)
        return attend(query_rows, key_part, value_part, key_mask, score_scale)
    new_attended = lax.map(critique_one, (by_head(new_queries), by_head(joined_keys), by_head(joined_values), head_lengths))
    new_attended = jnp.moveaxis(new_attended.reshape(ROWS, KV_HEADS, STEPS, group_size, HEAD), 1, 2).reshape(ROWS * STEPS, HEADS * HEAD)
    critique_out = finish(critique, new_attended, post_gain, o_weight)
    return (hidden_out, critique_out)
```

```python
import math

import jax
import jax.numpy as jnp
import numpy as np
from jax import lax
from jax.experimental import pallas as pl
from jax.experimental.pallas import tpu as pltpu
from jax.sharding import PartitionSpec as P

D = 4608
HEADS = 32
KV_HEADS = 16
HEAD = 128
ROWS = 4
SPAN = 128
WIDTH = 288
SLAB = 4 * WIDTH
HALF = WIDTH // 2
STEPS = 4

EPS = 1e-06
CAP = 50.0
BASE = 10000.0
SCALE = (D // HEADS) ** (-0.5)
F32 = jnp.float32
BF16 = jnp.bfloat16
MESH = pl.DeviceIdType.MESH
N_SEM = 160


def rope_table():
    freq = np.exp(np.arange(64, dtype=np.float64) * (-2.0 * math.log(BASE) / HEAD))
    angle = np.arange(2056, dtype=np.float64)[:, None] * freq
    return np.concatenate([np.cos(angle), np.sin(angle)], axis=-1).astype(np.float32)


def dot(a, b):
    return jnp.dot(a, b, preferred_element_type=F32)


def dot_t(a, b):
    return lax.dot_general(a, b, (((1,), (1,)), ((), ())), preferred_element_type=F32)


def kernel(
    hidden, critique, lengths, gains, table_hbm, wq, wk, wv, wo,
    out, c_out,
    xg, wraw, wt, gainb, pgb, xn, table, cosT, sinT, qbuf, kvg, attg, owslab, owt,
    pb, own, rs1, rs2, cg, cq, ckv, cattg, cpj, cown, crs, ssx, ssz,
    send_sem, recv_sem, local_sem,
):
    s = lax.axis_index("section")
    y = lax.axis_index("seq")
    h = lax.axis_index("head")
    x, z = h // 4, h % 4
    zlo, core = s // 2, s % 2

    def at_x(d):
        return {"head": ((x + d) % 4) * 4 + z}

    def at_z(d):
        return {"head": x * 4 + (z + d) % 4}

    def at_y(d):
        return {"seq": (y + d) % 4}

    to_zlo = {"section": (1 - zlo) * 2 + core}
    to_core = {"section": zlo * 2 + 1 - core}

    copies = {}

    def send(name, src, dst, device):
        i = len(copies)
        assert i < N_SEM
        copy = pltpu.make_async_remote_copy(
            src_ref=src, dst_ref=dst, send_sem=send_sem.at[i], recv_sem=recv_sem.at[i],
            device_id=device, device_id_type=MESH,
        )
        copy.start()
        copies[name] = copy

    def recv(name):
        copies[name].wait_recv()

    local = []

    def fetch(src, dst):
        copy = pltpu.make_async_copy(src, dst, local_sem.at[len(local)])
        copy.start()
        local.append(copy)
        return copy

    piece = pl.multiple_of(core * 128 + y * 32, 32)
    own_cols = pl.ds(pl.multiple_of(x * SLAB, 128), SLAB)
    fetch_w = [
        fetch(wq, wraw.at[:, 0:256]),
        fetch(wk, wraw.at[:, 256:384]),
        fetch(wv, wraw.at[:, 384:512]),
    ]
    fetch_table = fetch(table_hbm, table)
    fetch_o = fetch(wo.at[pl.ds(piece, 32), own_cols], owslab.at[0, pl.ds(piece, 32), :])

    def turn(value):
        return jnp.concatenate(
            [value[:, 0:128].T, value[:, 128:256].T, value[:, 256:288].T], axis=0
        )

    for r in range(ROWS):
        xg[r, 0, 0] = turn(hidden[r].astype(F32)).astype(BF16)
    c_rows = jnp.concatenate([critique[0].astype(F32), jnp.zeros((4, WIDTH), F32)], axis=0)
    c_pad = jnp.concatenate([c_rows[:, 256:288], jnp.zeros((8, 96), F32)], axis=1)
    cg[0, 0] = jnp.concatenate(
        [c_rows[:, 0:128], c_rows[:, 128:256], c_pad, jnp.zeros((8, 128), F32)], axis=0
    ).astype(BF16)

    ssx[0] = jnp.zeros((24, 128), F32)
    partners = [at_x(1), at_x(3), at_x(2), at_z(1), at_z(3), at_z(2), at_y(1), at_y(3), to_zlo, to_core]
    barrier = pltpu.get_barrier_semaphore()
    for partner in partners:
        pl.semaphore_signal(barrier, inc=1, device_id=partner, device_id_type=MESH)
    pl.semaphore_wait(barrier, len(partners))

    def z1(r):
        send(("z1", r, 0), xg.at[r, 0, 0], xg.at[r, 0, 3], at_z(1))
        send(("z1", r, 1), xg.at[r, 0, 0], xg.at[r, 0, 1], at_z(3))

    def x1a(r):
        send(("x1a", r, 0), xg.at[r, 0, 0], xg.at[r, 3, 0], at_x(1))
        send(("x1a", r, 1), xg.at[r, 0, 0], xg.at[r, 1, 0], at_x(3))

    def e1(r):
        recv(("z1", r, 0))
        send(("z2", r, 0), xg.at[r, 0, 3, 0:HALF], xg.at[r, 0, 2, 0:HALF], at_z(1))
        recv(("z1", r, 1))
        send(("z2", r, 1), xg.at[r, 0, 1, HALF:WIDTH], xg.at[r, 0, 2, HALF:WIDTH], at_z(3))

    def e2(r):
        recv(("z2", r, 0))
        recv(("z2", r, 1))
        send(("x1b", r, 0), xg.at[r, 0, 1:4], xg.at[r, 3, 1:4], at_x(1))
        send(("x1b", r, 1), xg.at[r, 0, 1:4], xg.at[r, 1, 1:4], at_x(3))

    def e3(r):
        recv(("x1a", r, 0))
        recv(("x1b", r, 0))
        send(("x2", r, 0), xg.at[r, 3, :, 0:HALF], xg.at[r, 2, :, 0:HALF], at_x(1))
        recv(("x1a", r, 1))
        recv(("x1b", r, 1))
        send(("x2", r, 1), xg.at[r, 1, :, HALF:WIDTH], xg.at[r, 2, :, HALF:WIDTH], at_x(3))

    def e4(r):
        recv(("x2", r, 0))
        recv(("x2", r, 1))

    def ow_x():
        for d in (1, 3, 2):
            cols = pl.ds(pl.multiple_of(((x + d) % 4) * SLAB, 128), SLAB)
            send(("ow", d), wo.at[pl.ds(piece, 32), cols], owslab.at[4 - d, pl.ds(piece, 32), :], at_x(d))

    def ow_y1():
        fetch_o.wait()
        for d in (1, 3, 2):
            recv(("ow", d))
        here = owslab.at[:, pl.ds(piece, 32), :]
        send("owy1r", here, here, at_y(1))
        send("owy1l", here, here, at_y(3))

    def ow_y2():
        low = pl.ds(pl.multiple_of(core * 128 + ((y + 3) % 4) * 32, 32), 16)
        high = pl.ds(pl.multiple_of(core * 128 + ((y + 1) % 4) * 32 + 16, 16), 16)
        recv("owy1r")
        send("owy2r", owslab.at[:, low, :], owslab.at[:, low, :], at_y(1))
        recv("owy1l")
        send("owy2l", owslab.at[:, high, :], owslab.at[:, high, :], at_y(3))

    def ow_core():
        recv("owy2r")
        recv("owy2l")
        half = owslab.at[:, pl.ds(pl.multiple_of(core * 128, 128), 128), :]
        send("owc", half, half, to_core)

    def ow_turn():
        recv("owc")

        def step(d, carry):
            turned = owslab[d].T
            for zz in range(4):
                row = pl.multiple_of(((zz - z + 4) % 4) * WIDTH, 32)
                owt[d, pl.ds(row, WIDTH), :] = turned[zz * WIDTH : (zz + 1) * WIDTH]
            return carry

        lax.fori_loop(0, 4, step, 0)

    def gain_tables():
        turned = gains[...].T
        for hh in range(16):
            for k in range(3):
                n = 128 if k < 2 else 32
                column = turned[0:n, hh * 3 + k : hh * 3 + k + 1]
                gainb[hh * WIDTH + k * 128 : hh * WIDTH + k * 128 + n, :] = jnp.broadcast_to(column, (n, 128))
        for k in range(3):
            n = 128 if k < 2 else 32
            pgb[k * 128 : k * 128 + n, :] = jnp.broadcast_to(turned[0:n, 48 + k : 49 + k], (n, 128))

    def rope_tables():
        fetch_table.wait()
        place = pl.multiple_of((s * 4 + y) * SPAN, SPAN)
        turned = table[pl.ds(place, SPAN), :].T
        cosT[...] = turned[0:64]
        sinT[...] = turned[64:128]

    def turn_weights(lo, hi):
        def step(c, carry):
            row = pl.multiple_of(c * 256, 256)
            wt[:, pl.ds(row, 256)] = wraw[pl.ds(row, 256), :].T
            return carry

        lax.fori_loop(lo, hi, step, 0)

    def source_head(b):
        return ((x + b // 4) % 4) * 4 + (z + b % 4) % 4

    def project(r):
        def squares(b, total):
            block = xg[r, b // 4, b % 4].astype(F32)
            return total + jnp.sum((block * block).reshape(WIDTH // 8, 8, 128), axis=0)

        total = lax.fori_loop(0, 16, squares, jnp.zeros((8, 128), F32))
        factor = lax.rsqrt(jnp.sum(total, axis=0, keepdims=True) / D + EPS)

        def scale(b, carry):
            rows = pl.ds(pl.multiple_of(source_head(b) * WIDTH, 32), WIDTH)
            block = xg[r, b // 4, b % 4].astype(F32)
            xn[rows, :] = (block * factor * gainb[rows, :]).astype(BF16)
            return carry

        lax.fori_loop(0, 16, scale, 0)
        qkv = dot(wt[...], xn[...])
        cosine, sine = cosT[...], sinT[...]

        def rotated(value):
            a, b = value[0:64], value[64:128]
            return jnp.concatenate([a * cosine - b * sine, b * cosine + a * sine], axis=0)

        qbuf[r, 0:128, :] = rotated(qkv[0:128]).T.astype(BF16)
        qbuf[r, 128:256, :] = rotated(qkv[128:256]).T.astype(BF16)
        kvg[r, 0, 0, 0, 0:128, :] = rotated(qkv[256:384]).astype(BF16)
        kvg[r, 0, 0, 0, 128:256, :] = qkv[384:512].astype(BF16)

    def kv1(r):
        send(("kv1", r), kvg.at[r, 0, 0, 0], kvg.at[r, 0, 0, 1], to_zlo)

    def kv2(r):
        recv(("kv1", r))
        send(("kv2", r, 0), kvg.at[r, 0, 0], kvg.at[r, 0, 3], at_y(1))
        send(("kv2", r, 1), kvg.at[r, 0, 0], kvg.at[r, 0, 1], at_y(3))

    def kv3(r):
        recv(("kv2", r, 0))
        send(("kv3", r, 0), kvg.at[r, 0, 3, 0], kvg.at[r, 0, 2, 0], at_y(1))
        recv(("kv2", r, 1))
        send(("kv3", r, 1), kvg.at[r, 0, 1, 1], kvg.at[r, 0, 2, 1], at_y(3))

    def kv4(r):
        recv(("kv3", r, 0))
        recv(("kv3", r, 1))
        send(("kv4", r), kvg.at[r, 0], kvg.at[r, 1], to_core)

    def key_start(b):
        dc, dy, dz = b // 8, (b // 2) % 4, b % 2
        section = ((zlo + dz) % 2) * 2 + (core + dc) % 2
        return (section * 4 + (y + dy) % 4) * SPAN

    def weigh(scores, keep):
        capped = CAP * jnp.tanh(scores * (SCALE / CAP))
        return jnp.where(keep, jnp.exp(capped), 0.0)

    def attend(r):
        recv(("kv4", r))
        queries = qbuf[r]
        length = lengths[r]
        first = (s * 4 + y) * SPAN
        token = first + lax.broadcasted_iota(jnp.int32, (256, 128), 0) % SPAN
        limit = jnp.minimum(token, length - 1)
        lane = lax.broadcasted_iota(jnp.int32, (256, 128), 1)

        def step(b, carry):
            num, den = carry
            keys = kvg.at[r, b // 8, (b // 2) % 4, b % 2]
            weight = weigh(dot(queries, keys[0:128, :]), lane + key_start(b) <= limit)
            return num + dot_t(weight.astype(BF16), keys[128:256, :]), den + weight

        zero = jnp.zeros((256, 128), F32)
        num, den = lax.fori_loop(0, 16, step, (zero, zero))
        result = num / jnp.sum(den, axis=-1, keepdims=True)
        attg[r, 0, :, 0:128] = result[0:128].astype(BF16)
        attg[r, 0, :, 128:256] = result[128:256].astype(BF16)

    def ax1(r):
        send(("ax1", r, 0), attg.at[r, 0], attg.at[r, 3], at_x(1))
        send(("ax1", r, 1), attg.at[r, 0], attg.at[r, 1], at_x(3))

    def ax2(r):
        recv(("ax1", r, 0))
        send(("ax2", r, 0), attg.at[r, 3, 0:64], attg.at[r, 2, 0:64], at_x(1))
        recv(("ax1", r, 1))
        send(("ax2", r, 1), attg.at[r, 1, 64:128], attg.at[r, 2, 64:128], at_x(3))

    def proj(r):
        recv(("ax2", r, 0))
        recv(("ax2", r, 1))
        for dz in (2, 1, 3, 0):
            rows = pl.ds(dz * WIDTH, WIDTH)
            part = dot_t(owt[0, rows, :], attg[r, 0])
            for d in range(1, 4):
                part = part + dot_t(owt[d, rows, :], attg[r, d])
            if dz:
                pb[r, dz] = part.astype(BF16)
            else:
                own[r] = part
            if dz == 2:
                send(("rs1", r, 0), pb.at[r, 2, 0:HALF], rs1.at[r, 0], at_z(1))
                send(("rs1", r, 1), pb.at[r, 2, HALF:WIDTH], rs1.at[r, 1], at_z(3))

    def rs_2(r):
        recv(("rs1", r, 0))
        pb[r, 1, 0:HALF] = (pb[r, 1, 0:HALF].astype(F32) + rs1[r, 0].astype(F32)).astype(BF16)
        send(("rs2", r, 0), pb.at[r, 1], rs2.at[r, 0], at_z(1))
        recv(("rs1", r, 1))
        pb[r, 3, HALF:WIDTH] = (pb[r, 3, HALF:WIDTH].astype(F32) + rs1[r, 1].astype(F32)).astype(BF16)
        send(("rs2", r, 1), pb.at[r, 3], rs2.at[r, 1], at_z(3))

    def rs_3(r):
        recv(("rs2", r, 0))
        recv(("rs2", r, 1))
        share = own[r] + rs2[r, 0].astype(F32) + rs2[r, 1].astype(F32)
        own[r] = share
        ssx[0, r : r + 1, :] = jnp.sum(share * share, axis=0, keepdims=True)

    def c_x():
        for d in (1, 3, 2):
            send(("cx", d), cg.at[0, 0], cg.at[0, 4 - d], at_x(d))

    def c_z():
        for d in (1, 3, 2):
            recv(("cx", d))
        for d in (1, 3, 2):
            send(("cz", d), cg.at[0], cg.at[4 - d], at_z(d))

    lane8 = lax.broadcasted_iota(jnp.int32, (8, 128), 1)

    def c_project():
        for d in (1, 3, 2):
            recv(("cz", d))

        def squares(b, total):
            block = cg[b // 4, b % 4].astype(F32)
            block = block * block
            return total + block[0:8] + block[8:16] + block[16:24]

        total = lax.fori_loop(0, 16, squares, jnp.zeros((8, 128), F32))
        factor = lax.rsqrt(jnp.sum(total, axis=-1, keepdims=True) / D + EPS)
        rest = jnp.zeros((8, 128), F32)

        def step(b, total):
            dz, dx = b // 4, b % 4
            head = ((x + dx) % 4) * 4 + (z + dz) % 4
            block = cg[dz, dx].astype(F32)
            row = pl.multiple_of(head * WIDTH, 32)
            for k in range(3):
                gain = gains[pl.ds(head * 3 + k, 1), :]
                part = block[k * 8 : k * 8 + 8] * factor * gain
                part = jnp.concatenate([part, rest], axis=0).astype(BF16)
                if k < 2:
                    total = total + dot(part, wraw[pl.ds(row + k * 128, 128), :])
                else:
                    total = total + dot(part[:, 0:32], wraw[pl.ds(row + 256, 32), :])
            return total

        qkv = lax.fori_loop(0, 16, step, jnp.zeros((16, 512), F32))[0:8]
        angles = table[pl.ds(lengths[y], 8), :]
        other = pltpu.roll(angles, 64, 1)
        front = lane8 < 64
        cosine = jnp.where(front, angles, other)
        sine = jnp.where(front, -other, angles)

        def rotated(value):
            return value * cosine + pltpu.roll(value, 64, 1) * sine

        cq[...] = jnp.concatenate([rotated(qkv[:, 0:128]), rotated(qkv[:, 128:256])], axis=0).astype(BF16)
        ckv[0] = jnp.concatenate([rotated(qkv[:, 256:384]), rest], axis=0).astype(BF16)
        ckv[1] = jnp.concatenate([qkv[:, 384:512], rest], axis=0).astype(BF16)

    def c_attend():
        queries = cq[...]
        length = lengths[y]
        lane = lax.broadcasted_iota(jnp.int32, (16, 128), 1)

        def step(b, carry):
            num, den = carry
            keys = kvg.at[y, b // 8, (b // 2) % 4, b % 2]
            weight = weigh(dot(queries, keys[0:128, :]), lane + key_start(b) < length)
            return num + dot_t(weight.astype(BF16), keys[128:256, :]), den + weight

        zero = jnp.zeros((16, 128), F32)
        num, den = lax.fori_loop(0, 16, step, (zero, zero))
        near = lax.broadcasted_iota(jnp.int32, (16, 16), 1) <= lax.broadcasted_iota(jnp.int32, (16, 16), 0) % 8
        weight = weigh(dot_t(queries, ckv[0]), near)
        num = num + dot(weight.astype(BF16), ckv[1])
        total = jnp.sum(den, axis=-1, keepdims=True) + jnp.sum(weight, axis=-1, keepdims=True)
        result = num / total
        rest = jnp.zeros((8, 128), F32)
        cattg[0, :, 0:128] = jnp.concatenate([result[0:8], rest], axis=0).astype(BF16)
        cattg[0, :, 128:256] = jnp.concatenate([result[8:16], rest], axis=0).astype(BF16)
        for d in (1, 3, 2):
            send(("ca", d), cattg.at[0], cattg.at[4 - d], at_x(d))

    def c_proj():
        for d in (1, 3, 2):
            recv(("ca", d))
        part = dot_t(cattg[0], owt[0])
        for d in range(1, 4):
            part = part + dot_t(cattg[d], owt[d])
        inside = lax.broadcasted_iota(jnp.int32, (16, 384), 1) < WIDTH
        for dz in range(4):
            moved = part if dz == 0 else pltpu.roll(part, SLAB - dz * WIDTH, 1)
            moved = jnp.where(inside, moved[:, 0:384], 0.0)
            if dz:
                cpj[dz] = moved.astype(BF16)
                send(("cr", dz), cpj.at[dz], crs.at[4 - dz], at_z(dz))
            else:
                cown[...] = moved

    def c_sum():
        share = cown[...]
        for d in (1, 3, 2):
            recv(("cr", d))
        for d in range(1, 4):
            share = share + crs[d].astype(F32)
        cown[...] = share
        ssx[0, 8:24, :] = jnp.broadcast_to(jnp.sum(share * share, axis=-1, keepdims=True), (16, 128))

    def finish():
        for d in (1, 3, 2):
            send(("sx", d), ssx.at[0], ssx.at[4 - d], at_x(d))
        for d in (1, 3, 2):
            recv(("sx", d))
        ssz[0] = (ssx[0] + ssx[1]) + (ssx[2] + ssx[3])
        for d in (1, 3, 2):
            send(("sz", d), ssz.at[0], ssz.at[4 - d], at_z(d))
        for d in (1, 3, 2):
            recv(("sz", d))
        factor = lax.rsqrt(((ssz[0] + ssz[1]) + (ssz[2] + ssz[3])) / D + EPS)
        for r in range(ROWS):
            part = own[r] * factor[r : r + 1, :] * pgb[...]
            for k in range(3):
                lo, hi = k * 128, min(k * 128 + 128, WIDTH)
                out[r, :, lo:hi] = (hidden[r, :, lo:hi].astype(F32) + part[lo:hi].T).astype(BF16)
        for k in range(3):
            lo, hi = k * 128, min(k * 128 + 128, WIDTH)
            part = cown[0:4, k * 128 : k * 128 + 128] * factor[8:12, :] * gains[48 + k : 49 + k, :]
            c_out[0, :, lo:hi] = (critique[0, :, lo:hi].astype(F32) + part[:, 0 : hi - lo]).astype(BF16)

    z1(0)
    x1a(0)
    z1(1)
    ow_x()
    c_x()
    x1a(1)
    gain_tables()
    rope_tables()
    e1(0)
    z1(2)
    for copy in fetch_w:
        copy.wait()
    turn_weights(0, 6)
    e2(0)
    x1a(2)
    e1(1)
    z1(3)
    c_z()
    turn_weights(6, 12)
    e2(1)
    x1a(3)
    ow_y1()
    turn_weights(12, 18)
    e1(2)
    c_project()
    e3(0)
    e2(2)
    e1(3)
    ow_y2()
    e4(0)
    project(0)
    kv1(0)
    e3(1)
    e2(3)
    ow_core()
    kv2(0)
    kv3(0)
    e4(1)
    project(1)
    kv1(1)
    e3(2)
    kv4(0)
    ow_turn()
    kv2(1)
    attend(0)
    ax1(0)
    kv3(1)
    e4(2)
    project(2)
    kv1(2)
    e3(3)
    ax2(0)
    kv4(1)
    kv2(2)
    attend(1)
    ax1(1)
    kv3(2)
    proj(0)
    e4(3)
    project(3)
    kv1(3)
    kv4(2)
    rs_2(0)
    ax2(1)
    kv2(3)
    attend(2)
    ax1(2)
    kv3(3)
    proj(1)
    rs_3(0)
    kv4(3)
    ax2(2)
    rs_2(1)
    proj(2)
    attend(3)
    ax1(3)
    rs_3(1)
    c_attend()
    ax2(3)
    rs_2(2)
    proj(3)
    c_proj()
    rs_3(2)
    rs_2(3)
    c_sum()
    rs_3(3)
    finish()
    for copy in copies.values():
        copy.wait_send()


def body(hidden, critique, lengths, pre_gain, post_gain, q_weight, k_weight, v_weight, o_weight):
    pre = jnp.pad(pre_gain.astype(F32).reshape(16, WIDTH), ((0, 0), (0, 384 - WIDTH))).reshape(48, 128)
    post = jnp.pad(post_gain.astype(F32), (0, 384 - WIDTH)).reshape(3, 128)
    gains = jnp.concatenate([pre, post, jnp.zeros((77, 128), F32)], axis=0)
    table = jnp.asarray(rope_table())
    vmem = pl.BlockSpec(memory_space=pltpu.VMEM)
    smem = pl.BlockSpec(memory_space=pltpu.SMEM)
    anywhere = pl.BlockSpec(memory_space=pl.ANY)
    return pl.pallas_call(
        kernel,
        out_shape=(
            jax.ShapeDtypeStruct(hidden.shape, BF16),
            jax.ShapeDtypeStruct(critique.shape, BF16),
        ),
        in_specs=[vmem, vmem, smem, vmem, anywhere, anywhere, anywhere, anywhere, anywhere],
        out_specs=(vmem, vmem),
        scratch_shapes=[
            pltpu.VMEM((ROWS, 4, 4, WIDTH, SPAN), BF16),
            pltpu.VMEM((D, 512), BF16),
            pltpu.VMEM((512, D), BF16),
            pltpu.VMEM((D, 128), F32),
            pltpu.VMEM((WIDTH, 128), F32),
            pltpu.VMEM((D, SPAN), BF16),
            pltpu.VMEM((2056, 128), F32),
            pltpu.VMEM((64, SPAN), F32),
            pltpu.VMEM((64, SPAN), F32),
            pltpu.VMEM((ROWS, 256, HEAD), BF16),
            pltpu.VMEM((ROWS, 2, 4, 2, 256, SPAN), BF16),
            pltpu.VMEM((ROWS, 4, SPAN, 256), BF16),
            pltpu.VMEM((4, 256, SLAB), BF16),
            pltpu.VMEM((4, SLAB, 256), BF16),
            pltpu.VMEM((ROWS, 4, WIDTH, SPAN), BF16),
            pltpu.VMEM((ROWS, WIDTH, SPAN), F32),
            pltpu.VMEM((ROWS, 2, HALF, SPAN), BF16),
            pltpu.VMEM((ROWS, 2, WIDTH, SPAN), BF16),
            pltpu.VMEM((4, 4, 32, 128), BF16),
            pltpu.VMEM((16, 128), BF16),
            pltpu.VMEM((2, 16, 128), BF16),
            pltpu.VMEM((4, 16, 256), BF16),
            pltpu.VMEM((4, 16, 384), BF16),
            pltpu.VMEM((16, 384), F32),
            pltpu.VMEM((4, 16, 384), BF16),
            pltpu.VMEM((4, 24, 128), F32),
            pltpu.VMEM((4, 24, 128), F32),
            pltpu.SemaphoreType.DMA((N_SEM,)),
            pltpu.SemaphoreType.DMA((N_SEM,)),
            pltpu.SemaphoreType.DMA((8,)),
        ],
        compiler_params=pltpu.CompilerParams(
            collective_id=0, has_side_effects=True, vmem_limit_bytes=56 * 1024 * 1024
        ),
        cost_estimate=pl.CostEstimate(flops=5_000_000_000, bytes_accessed=16_000_000, transcendentals=4_000_000),
    )(hidden, critique, lengths, gains, table, q_weight, k_weight, v_weight, o_weight)


def solution(mesh):
    return jax.shard_map(
        body,
        mesh=mesh,
        in_specs=(
            P(None, ("section", "seq"), "head"),
            P("seq", None, "head"),
            P(),
            P(),
            P("head"),
            P(None, "head"),
            P(None, "head"),
            P(None, "head"),
            P("head", None),
        ),
        out_specs=(P(None, ("section", "seq"), "head"), P("seq", None, "head")),
        check_vma=False,
    )
```

```python
import math

import jax
import jax.numpy as jnp
import numpy as np
from jax import lax
from jax.experimental import pallas as pl
from jax.experimental.pallas import tpu as pltpu
from jax.sharding import PartitionSpec as P

D = 4608
HEADS = 32
KV_HEADS = 16
HEAD = 128
ROWS = 4
SPAN = 128
WIDTH = 288
SLAB = 4 * WIDTH
HALF = WIDTH // 2
STEPS = 4

EPS = 1e-06
CAP = 50.0
BASE = 10000.0
SCALE = (D // HEADS) ** (-0.5)
F32 = jnp.float32
BF16 = jnp.bfloat16
MESH = pl.DeviceIdType.MESH
N_SEM = 192


def rope_table():
    freq = np.exp(np.arange(64, dtype=np.float64) * (-2.0 * math.log(BASE) / HEAD))
    angle = np.arange(2056, dtype=np.float64)[:, None] * freq
    return np.concatenate([np.cos(angle), np.sin(angle)], axis=-1).astype(np.float32)


def dot(a, b):
    return jnp.dot(a, b, preferred_element_type=F32)


def dot_t(a, b):
    return lax.dot_general(a, b, (((1,), (1,)), ((), ())), preferred_element_type=F32)


def kernel(
    hidden, critique, lengths, gains, table_hbm, wq, wk, wv, wo,
    out, c_out,
    xg, wraw, wt, pgb, table, cosT, sinT, qbuf, kvg, attg, owslab, owt,
    pb, own, rs1, rs2, cg, cq, ckv, cattg, cpj, cown, crs, ssx, ssz, prex, prez, fac,
    send_sem, recv_sem, local_sem,
):
    s = lax.axis_index("section")
    y = lax.axis_index("seq")
    h = lax.axis_index("head")
    x, z = h // 4, h % 4
    zlo, core = s // 2, s % 2

    def at_x(d):
        return {"head": ((x + d) % 4) * 4 + z}

    def at_z(d):
        return {"head": x * 4 + (z + d) % 4}

    def at_y(d):
        return {"seq": (y + d) % 4}

    to_zlo = {"section": (1 - zlo) * 2 + core}
    to_core = {"section": zlo * 2 + 1 - core}

    copies = {}

    def send(name, src, dst, device):
        i = len(copies)
        assert i < N_SEM
        copy = pltpu.make_async_remote_copy(
            src_ref=src, dst_ref=dst, send_sem=send_sem.at[i], recv_sem=recv_sem.at[i],
            device_id=device, device_id_type=MESH,
        )
        copy.start()
        copies[name] = copy

    def recv(name):
        copies[name].wait_recv()

    local = []

    def fetch(src, dst):
        copy = pltpu.make_async_copy(src, dst, local_sem.at[len(local)])
        copy.start()
        local.append(copy)
        return copy

    piece = pl.multiple_of(core * 128 + y * 32, 32)
    own_cols = pl.ds(pl.multiple_of(x * SLAB, 128), SLAB)
    fetch_w = [
        fetch(wq, wraw.at[:, 0:256]),
        fetch(wk, wraw.at[:, 256:384]),
        fetch(wv, wraw.at[:, 384:512]),
    ]
    fetch_table = fetch(table_hbm, table)
    fetch_o = fetch(wo.at[pl.ds(piece, 32), own_cols], owslab.at[0, pl.ds(piece, 32), :])

    def column(row, k):
        n = 128 if k < 2 else 32
        return jnp.broadcast_to(gains[:, k * 128 : k * 128 + 128].T[0:n, row : row + 1], (n, 128))

    gain = jnp.concatenate([column(0, k) for k in range(3)], axis=0)
    for r in range(ROWS):
        block = hidden[r].astype(F32)
        xg[r, x, z] = (block * gain).astype(BF16)
        prex[0, r : r + 1, :] = jnp.sum(block * block, axis=0, keepdims=True)
    c_rows = jnp.concatenate([critique[0].astype(F32), jnp.zeros((12, WIDTH), F32)], axis=0)
    c_sums = jnp.sum(c_rows * c_rows, axis=-1, keepdims=True)
    prex[0, 4:8, :] = jnp.zeros((4, 128), F32)
    prex[0, 8:16, :] = jnp.broadcast_to(c_sums[0:8], (8, 128))
    c_rows = c_rows * gains[0:1, 0:WIDTH]
    c_last = jnp.concatenate([c_rows[:, 256:288], jnp.zeros((16, 96), F32)], axis=1)
    cg[0, 0] = jnp.concatenate([c_rows[:, 0:128], c_rows[:, 128:256], c_last], axis=0).astype(BF16)

    ssx[0] = jnp.zeros((24, 128), F32)
    partners = [at_x(1), at_x(3), at_x(2), at_z(1), at_z(3), at_z(2), at_y(1), at_y(3), to_zlo, to_core]
    barrier = pltpu.get_barrier_semaphore()
    for partner in partners:
        pl.semaphore_signal(barrier, inc=1, device_id=partner, device_id_type=MESH)
    pl.semaphore_wait(barrier, len(partners))

    zr, zl, zo = (z + 1) % 4, (z + 3) % 4, (z + 2) % 4
    xr, xl, xo = (x + 1) % 4, (x + 3) % 4, (x + 2) % 4
    first_half, last_half = pl.ds(0, HALF), pl.ds(HALF, HALF)

    def z1(r):
        block = xg.at[r, x, z]
        send(("z1", r, 0), block, block, at_z(1))
        send(("z1", r, 1), block, block, at_z(3))

    def x1(r, k, place):
        block = xg.at[r, x, place]
        send(("x1", r, k, 0), block, block, at_x(1))
        send(("x1", r, k, 1), block, block, at_x(3))

    def x1a(r):
        x1(r, 0, z)

    def e1(r):
        recv(("z1", r, 0))
        half = xg.at[r, x, zl, first_half]
        send(("z2", r, 0), half, half, at_z(1))
        recv(("z1", r, 1))
        half = xg.at[r, x, zr, last_half]
        send(("z2", r, 1), half, half, at_z(3))
        x1(r, 1, zl)
        x1(r, 3, zr)

    def e2(r):
        recv(("z2", r, 0))
        recv(("z2", r, 1))
        x1(r, 2, zo)

    def e3(r):
        for k in range(4):
            recv(("x1", r, k, 0))
        half = xg.at[r, xl, :, first_half]
        send(("x2", r, 0), half, half, at_x(1))
        for k in range(4):
            recv(("x1", r, k, 1))
        half = xg.at[r, xr, :, last_half]
        send(("x2", r, 1), half, half, at_x(3))

    def e4(r):
        recv(("x2", r, 0))
        recv(("x2", r, 1))

    def ow_x():
        for d in (1, 3, 2):
            cols = pl.ds(pl.multiple_of(((x + d) % 4) * SLAB, 128), SLAB)
            send(("ow", d), wo.at[pl.ds(piece, 32), cols], owslab.at[4 - d, pl.ds(piece, 32), :], at_x(d))

    def ow_y1():
        fetch_o.wait()
        for d in (1, 3, 2):
            recv(("ow", d))
        here = owslab.at[:, pl.ds(piece, 32), :]
        send("owy1r", here, here, at_y(1))
        send("owy1l", here, here, at_y(3))

    def ow_y2():
        low = pl.ds(pl.multiple_of(core * 128 + ((y + 3) % 4) * 32, 32), 16)
        high = pl.ds(pl.multiple_of(core * 128 + ((y + 1) % 4) * 32 + 16, 16), 16)
        recv("owy1r")
        send("owy2r", owslab.at[:, low, :], owslab.at[:, low, :], at_y(1))
        recv("owy1l")
        send("owy2l", owslab.at[:, high, :], owslab.at[:, high, :], at_y(3))

    def ow_core():
        recv("owy2r")
        recv("owy2l")
        half = owslab.at[:, pl.ds(pl.multiple_of(core * 128, 128), 128), :]
        send("owc", half, half, to_core)

    def ow_turn():
        recv("owc")

        def step(d, carry):
            turned = owslab[d].T
            for zz in range(4):
                row = pl.multiple_of(((zz - z + 4) % 4) * WIDTH, 32)
                owt[d, pl.ds(row, WIDTH), :] = turned[zz * WIDTH : (zz + 1) * WIDTH]
            return carry

        lax.fori_loop(0, 4, step, 0)

    def gain_tables():
        for k in range(3):
            pgb[k * 128 : min(k * 128 + 128, WIDTH), :] = column(1, k)

    def rope_tables():
        fetch_table.wait()
        place = pl.multiple_of((s * 4 + y) * SPAN, SPAN)
        turned = table[pl.ds(place, SPAN), :].T
        cosT[...] = turned[0:64]
        sinT[...] = turned[64:128]

    def turn_weights(lo, hi):
        def step(c, carry):
            row = pl.multiple_of(c * 256, 256)
            wt[:, pl.ds(row, 256)] = wraw[pl.ds(row, 256), :].T
            return carry

        lax.fori_loop(lo, hi, step, 0)

    def pre_x():
        for d in (1, 3, 2):
            send(("px", d), prex.at[0], prex.at[4 - d], at_x(d))

    def pre_z():
        for d in (1, 3, 2):
            recv(("px", d))
        prez[0] = (prex[0] + prex[1]) + (prex[2] + prex[3])
        for d in (1, 3, 2):
            send(("pz", d), prez.at[0], prez.at[4 - d], at_z(d))

    def pre_done():
        for d in (1, 3, 2):
            recv(("pz", d))
        fac[...] = lax.rsqrt(((prez[0] + prez[1]) + (prez[2] + prez[3])) / D + EPS)

    def project(r):
        qkv = dot(wt[...], xg[r].reshape(D, SPAN)) * fac[r : r + 1, :]
        cosine, sine = cosT[...], sinT[...]

        def rotated(value):
            a, b = value[0:64], value[64:128]
            return jnp.concatenate([a * cosine - b * sine, b * cosine + a * sine], axis=0)

        qbuf[r, 0:128, :] = rotated(qkv[0:128]).T.astype(BF16)
        qbuf[r, 128:256, :] = rotated(qkv[128:256]).T.astype(BF16)
        kvg[r, 0, 0, 0, 0:128, :] = rotated(qkv[256:384]).astype(BF16)
        kvg[r, 0, 0, 0, 128:256, :] = qkv[384:512].astype(BF16)

    def kv1(r):
        send(("kv1", r), kvg.at[r, 0, 0, 0], kvg.at[r, 0, 0, 1], to_zlo)

    def kv2(r):
        recv(("kv1", r))
        send(("kv2", r, 0), kvg.at[r, 0, 0], kvg.at[r, 0, 3], at_y(1))
        send(("kv2", r, 1), kvg.at[r, 0, 0], kvg.at[r, 0, 1], at_y(3))

    def kv3(r):
        recv(("kv2", r, 0))
        send(("kv3", r, 0), kvg.at[r, 0, 3, 0], kvg.at[r, 0, 2, 0], at_y(1))
        recv(("kv2", r, 1))
        send(("kv3", r, 1), kvg.at[r, 0, 1, 1], kvg.at[r, 0, 2, 1], at_y(3))

    def kv4(r):
        recv(("kv3", r, 0))
        recv(("kv3", r, 1))
        send(("kv4", r), kvg.at[r, 0], kvg.at[r, 1], to_core)

    def key_start(b):
        dc, dy, dz = b // 8, (b // 2) % 4, b % 2
        section = ((zlo + dz) % 2) * 2 + (core + dc) % 2
        return (section * 4 + (y + dy) % 4) * SPAN

    def weigh(scores, keep):
        capped = CAP * jnp.tanh(scores * (SCALE / CAP))
        return jnp.where(keep, jnp.exp(capped), 0.0)

    def attend(r):
        recv(("kv4", r))
        queries = qbuf[r]
        length = lengths[r]
        first = (s * 4 + y) * SPAN
        token = first + lax.broadcasted_iota(jnp.int32, (256, 128), 0) % SPAN
        limit = jnp.minimum(token, length - 1)
        lane = lax.broadcasted_iota(jnp.int32, (256, 128), 1)

        def step(b, carry):
            num, den = carry
            for i in range(4):
                keys = kvg.at[r, b // 2, (b % 2) * 2 + i // 2, i % 2]
                weight = weigh(dot(queries, keys[0:128, :]), lane + key_start(b * 4 + i) <= limit)
                num = num + dot_t(weight.astype(BF16), keys[128:256, :])
                den = den + weight
            return num, den

        zero = jnp.zeros((256, 128), F32)
        num, den = lax.fori_loop(0, 4, step, (zero, zero))
        result = num / jnp.sum(den, axis=-1, keepdims=True)
        attg[r, 0, :, 0:128] = result[0:128].astype(BF16)
        attg[r, 0, :, 128:256] = result[128:256].astype(BF16)

    def ax1(r):
        send(("ax1", r, 0), attg.at[r, 0], attg.at[r, 3], at_x(1))
        send(("ax1", r, 1), attg.at[r, 0], attg.at[r, 1], at_x(3))

    def ax2(r):
        recv(("ax1", r, 0))
        send(("ax2", r, 0), attg.at[r, 3, 0:64], attg.at[r, 2, 0:64], at_x(1))
        recv(("ax1", r, 1))
        send(("ax2", r, 1), attg.at[r, 1, 64:128], attg.at[r, 2, 64:128], at_x(3))

    def proj(r):
        recv(("ax2", r, 0))
        recv(("ax2", r, 1))
        for dz in (2, 1, 3, 0):
            rows = pl.ds(dz * WIDTH, WIDTH)
            part = dot_t(owt[0, rows, :], attg[r, 0])
            for d in range(1, 4):
                part = part + dot_t(owt[d, rows, :], attg[r, d])
            if dz:
                pb[r, dz] = part.astype(BF16)
            else:
                own[r] = part
            if dz == 2:
                send(("rs1", r, 0), pb.at[r, 2, 0:HALF], rs1.at[r, 0], at_z(1))
                send(("rs1", r, 1), pb.at[r, 2, HALF:WIDTH], rs1.at[r, 1], at_z(3))

    def rs_2(r):
        recv(("rs1", r, 0))
        pb[r, 1, 0:HALF] = (pb[r, 1, 0:HALF].astype(F32) + rs1[r, 0].astype(F32)).astype(BF16)
        send(("rs2", r, 0), pb.at[r, 1], rs2.at[r, 0], at_z(1))
        recv(("rs1", r, 1))
        pb[r, 3, HALF:WIDTH] = (pb[r, 3, HALF:WIDTH].astype(F32) + rs1[r, 1].astype(F32)).astype(BF16)
        send(("rs2", r, 1), pb.at[r, 3], rs2.at[r, 1], at_z(3))

    def rs_3(r):
        recv(("rs2", r, 0))
        recv(("rs2", r, 1))
        share = own[r] + rs2[r, 0].astype(F32) + rs2[r, 1].astype(F32)
        own[r] = share
        ssx[0, r : r + 1, :] = jnp.sum(share * share, axis=0, keepdims=True)

    def c_x():
        for d in (1, 3, 2):
            send(("cx", d), cg.at[0, 0], cg.at[0, 4 - d], at_x(d))

    def c_z():
        for d in (1, 3, 2):
            recv(("cx", d))
        for d in (1, 3, 2):
            send(("cz", d), cg.at[0], cg.at[4 - d], at_z(d))

    lane8 = lax.broadcasted_iota(jnp.int32, (8, 128), 1)

    def c_project():
        for d in (1, 3, 2):
            recv(("cz", d))

        def step(dz, total):
            for dx in range(4):
                head = ((x + dx) % 4) * 4 + (z + dz) % 4
                row = pl.multiple_of(head * WIDTH, 32)
                total = total + dot(cg[dz, dx, 0:16], wraw[pl.ds(row, 128), :])
                total = total + dot(cg[dz, dx, 16:32], wraw[pl.ds(row + 128, 128), :])
                total = total + dot(cg[dz, dx, 32:48, 0:32], wraw[pl.ds(row + 256, 32), :])
            return total

        qkv = lax.fori_loop(0, 4, step, jnp.zeros((16, 512), F32))[0:8] * fac[8:16, 0:1]
        rest = jnp.zeros((8, 128), F32)
        angles = table[pl.ds(lengths[y], 8), :]
        other = pltpu.roll(angles, 64, 1)
        front = lane8 < 64
        cosine = jnp.where(front, angles, other)
        sine = jnp.where(front, -other, angles)

        def rotated(value):
            return value * cosine + pltpu.roll(value, 64, 1) * sine

        cq[...] = jnp.concatenate([rotated(qkv[:, 0:128]), rotated(qkv[:, 128:256])], axis=0).astype(BF16)
        ckv[0] = jnp.concatenate([rotated(qkv[:, 256:384]), rest], axis=0).astype(BF16)
        ckv[1] = jnp.concatenate([qkv[:, 384:512], rest], axis=0).astype(BF16)

    def c_attend():
        queries = cq[...]
        length = lengths[y]
        lane = lax.broadcasted_iota(jnp.int32, (16, 128), 1)

        num = jnp.zeros((16, 128), F32)
        den = jnp.zeros((16, 128), F32)
        for b in range(16):
            keys = kvg.at[y, b // 8, (b // 2) % 4, b % 2]
            weight = weigh(dot(queries, keys[0:128, :]), lane + key_start(b) < length)
            num = num + dot_t(weight.astype(BF16), keys[128:256, :])
            den = den + weight
        near = lax.broadcasted_iota(jnp.int32, (16, 16), 1) <= lax.broadcasted_iota(jnp.int32, (16, 16), 0) % 8
        weight = weigh(dot_t(queries, ckv[0]), near)
        num = num + dot(weight.astype(BF16), ckv[1])
        total = jnp.sum(den, axis=-1, keepdims=True) + jnp.sum(weight, axis=-1, keepdims=True)
        result = num / total
        rest = jnp.zeros((8, 128), F32)
        cattg[0, :, 0:128] = jnp.concatenate([result[0:8], rest], axis=0).astype(BF16)
        cattg[0, :, 128:256] = jnp.concatenate([result[8:16], rest], axis=0).astype(BF16)
        for d in (1, 3, 2):
            send(("ca", d), cattg.at[0], cattg.at[4 - d], at_x(d))

    def c_proj():
        for d in (1, 3, 2):
            recv(("ca", d))
        part = dot_t(cattg[0], owt[0])
        for d in range(1, 4):
            part = part + dot_t(cattg[d], owt[d])
        inside = lax.broadcasted_iota(jnp.int32, (16, 384), 1) < WIDTH
        for dz in range(4):
            moved = part if dz == 0 else pltpu.roll(part, SLAB - dz * WIDTH, 1)
            moved = jnp.where(inside, moved[:, 0:384], 0.0)
            if dz:
                cpj[dz] = moved.astype(BF16)
                send(("cr", dz), cpj.at[dz], crs.at[4 - dz], at_z(dz))
            else:
                cown[...] = moved

    def c_sum():
        share = cown[...]
        for d in (1, 3, 2):
            recv(("cr", d))
        for d in range(1, 4):
            share = share + crs[d].astype(F32)
        cown[...] = share
        ssx[0, 8:24, :] = jnp.broadcast_to(jnp.sum(share * share, axis=-1, keepdims=True), (16, 128))

    def finish():
        for d in (1, 3, 2):
            send(("sx", d), ssx.at[0], ssx.at[4 - d], at_x(d))
        for d in (1, 3, 2):
            recv(("sx", d))
        ssz[0] = (ssx[0] + ssx[1]) + (ssx[2] + ssx[3])
        for d in (1, 3, 2):
            send(("sz", d), ssz.at[0], ssz.at[4 - d], at_z(d))
        for d in (1, 3, 2):
            recv(("sz", d))
        factor = lax.rsqrt(((ssz[0] + ssz[1]) + (ssz[2] + ssz[3])) / D + EPS)
        for r in range(ROWS):
            part = own[r] * factor[r : r + 1, :] * pgb[...]
            out[r] = (hidden[r].astype(F32) + part).astype(BF16)
        for k in range(3):
            lo, hi = k * 128, min(k * 128 + 128, WIDTH)
            part = cown[0:4, k * 128 : k * 128 + 128] * factor[8:12, :] * gains[1:2, k * 128 : k * 128 + 128]
            c_out[0, :, lo:hi] = (critique[0, :, lo:hi].astype(F32) + part[:, 0 : hi - lo]).astype(BF16)

    pre_x()
    z1(0)
    x1a(0)
    c_x()
    z1(1)
    ow_x()
    x1a(1)
    gain_tables()
    rope_tables()
    e1(0)
    z1(2)
    for copy in fetch_w:
        copy.wait()
    turn_weights(0, 6)
    e2(0)
    x1a(2)
    e1(1)
    z1(3)
    pre_z()
    c_z()
    turn_weights(6, 12)
    e2(1)
    x1a(3)
    ow_y1()
    turn_weights(12, 18)
    e1(2)
    pre_done()
    e3(0)
    c_project()
    e2(2)
    e1(3)
    ow_y2()
    e4(0)
    project(0)
    kv1(0)
    e3(1)
    e2(3)
    ow_core()
    kv2(0)
    kv3(0)
    e4(1)
    project(1)
    kv1(1)
    e3(2)
    kv4(0)
    ow_turn()
    kv2(1)
    attend(0)
    ax1(0)
    kv3(1)
    e4(2)
    project(2)
    kv1(2)
    e3(3)
    ax2(0)
    kv4(1)
    kv2(2)
    attend(1)
    ax1(1)
    kv3(2)
    proj(0)
    e4(3)
    project(3)
    kv1(3)
    kv4(2)
    rs_2(0)
    ax2(1)
    kv2(3)
    attend(2)
    ax1(2)
    kv3(3)
    proj(1)
    rs_3(0)
    kv4(3)
    ax2(2)
    rs_2(1)
    proj(2)
    attend(3)
    ax1(3)
    rs_3(1)
    c_attend()
    ax2(3)
    rs_2(2)
    proj(3)
    c_proj()
    rs_3(2)
    rs_2(3)
    c_sum()
    rs_3(3)
    finish()
    for copy in copies.values():
        copy.wait_send()


def body(hidden, critique, lengths, pre_gain, post_gain, q_weight, k_weight, v_weight, o_weight):
    own_gain = lax.dynamic_slice(pre_gain, (lax.axis_index("head") * WIDTH,), (WIDTH,))
    gains = jnp.pad(jnp.stack([own_gain, post_gain]).astype(F32), ((0, 6), (0, 384 - WIDTH)))
    table = jnp.asarray(rope_table())
    vmem = pl.BlockSpec(memory_space=pltpu.VMEM)
    smem = pl.BlockSpec(memory_space=pltpu.SMEM)
    anywhere = pl.BlockSpec(memory_space=pl.ANY)
    turned = jnp.transpose(hidden, (0, 2, 1))
    result, c_result = pl.pallas_call(
        kernel,
        out_shape=(
            jax.ShapeDtypeStruct(turned.shape, BF16),
            jax.ShapeDtypeStruct(critique.shape, BF16),
        ),
        in_specs=[vmem, vmem, smem, vmem, anywhere, anywhere, anywhere, anywhere, anywhere],
        out_specs=(vmem, vmem),
        scratch_shapes=[
            pltpu.VMEM((ROWS, 4, 4, WIDTH, SPAN), BF16),
            pltpu.VMEM((D, 512), BF16),
            pltpu.VMEM((512, D), BF16),
            pltpu.VMEM((WIDTH, 128), F32),
            pltpu.VMEM((2056, 128), F32),
            pltpu.VMEM((64, SPAN), F32),
            pltpu.VMEM((64, SPAN), F32),
            pltpu.VMEM((ROWS, 256, HEAD), BF16),
            pltpu.VMEM((ROWS, 2, 4, 2, 256, SPAN), BF16),
            pltpu.VMEM((ROWS, 4, SPAN, 256), BF16),
            pltpu.VMEM((4, 256, SLAB), BF16),
            pltpu.VMEM((4, SLAB, 256), BF16),
            pltpu.VMEM((ROWS, 4, WIDTH, SPAN), BF16),
            pltpu.VMEM((ROWS, WIDTH, SPAN), F32),
            pltpu.VMEM((ROWS, 2, HALF, SPAN), BF16),
            pltpu.VMEM((ROWS, 2, WIDTH, SPAN), BF16),
            pltpu.VMEM((4, 4, 48, 128), BF16),
            pltpu.VMEM((16, 128), BF16),
            pltpu.VMEM((2, 16, 128), BF16),
            pltpu.VMEM((4, 16, 256), BF16),
            pltpu.VMEM((4, 16, 384), BF16),
            pltpu.VMEM((16, 384), F32),
            pltpu.VMEM((4, 16, 384), BF16),
            pltpu.VMEM((4, 24, 128), F32),
            pltpu.VMEM((4, 24, 128), F32),
            pltpu.VMEM((4, 16, 128), F32),
            pltpu.VMEM((4, 16, 128), F32),
            pltpu.VMEM((16, 128), F32),
            pltpu.SemaphoreType.DMA((N_SEM,)),
            pltpu.SemaphoreType.DMA((N_SEM,)),
            pltpu.SemaphoreType.DMA((8,)),
        ],
        compiler_params=pltpu.CompilerParams(
            collective_id=0, has_side_effects=True, vmem_limit_bytes=56 * 1024 * 1024
        ),
        cost_estimate=pl.CostEstimate(flops=5_000_000_000, bytes_accessed=16_000_000, transcendentals=4_000_000),
    )(turned, critique, lengths, gains, table, q_weight, k_weight, v_weight, o_weight)
    return jnp.transpose(result, (0, 2, 1)), c_result


def solution(mesh):
    return jax.shard_map(
        body,
        mesh=mesh,
        in_specs=(
            P(None, ("section", "seq"), "head"),
            P("seq", None, "head"),
            P(),
            P(),
            P("head"),
            P(None, "head"),
            P(None, "head"),
            P(None, "head"),
            P("head", None),
        ),
        out_specs=(P(None, ("section", "seq"), "head"), P("seq", None, "head")),
        check_vma=False,
    )
```

```python
import math

import jax
import jax.numpy as jnp
import numpy as np
from jax import lax
from jax.experimental import pallas as pl
from jax.experimental.pallas import tpu as pltpu
from jax.sharding import PartitionSpec as P

D = 4608
HEADS = 32
KV_HEADS = 16
HEAD = 128
ROWS = 4
SPAN = 128
WIDTH = 288
SLAB = 4 * WIDTH
HALF = WIDTH // 2
FIRST = 240
STEPS = 4

EPS = 1e-06
CAP = 50.0
BASE = 10000.0
SCALE = (D // HEADS) ** (-0.5)
F32 = jnp.float32
BF16 = jnp.bfloat16
MESH = pl.DeviceIdType.MESH
N_SEM = 232


def rope_table():
    freq = np.exp(np.arange(64, dtype=np.float64) * (-2.0 * math.log(BASE) / HEAD))
    angle = np.arange(2056, dtype=np.float64)[:, None] * freq
    return np.concatenate([np.cos(angle), np.sin(angle)], axis=-1).astype(np.float32)


def dot(a, b):
    return jnp.dot(a, b, preferred_element_type=F32)


def dot_t(a, b):
    return lax.dot_general(a, b, (((1,), (1,)), ((), ())), preferred_element_type=F32)


def kernel(
    hidden, critique, lengths, gains, table_hbm, wq, wk, wv, wo,
    out, c_out,
    xg, wraw, wt, pgb, table, cosT, sinT, qbuf, kvg, attg, owslab, owt,
    pb, own, rs1, rs2, cg, cq, ckv, cattg, cpj, cown, crs, ssx, ssz, prex, prez, fac,
    send_sem, recv_sem, local_sem,
):
    s = lax.axis_index("section")
    y = lax.axis_index("seq")
    h = lax.axis_index("head")
    x, z = h // 4, h % 4
    zlo, core = s // 2, s % 2

    def at_x(d):
        return {"head": ((x + d) % 4) * 4 + z}

    def at_z(d):
        return {"head": x * 4 + (z + d) % 4}

    def at_y(d):
        return {"seq": (y + d) % 4}

    to_zlo = {"section": (1 - zlo) * 2 + core}
    to_core = {"section": zlo * 2 + 1 - core}

    partners = [at_x(1), at_x(3), at_x(2), at_z(1), at_z(3), at_z(2), at_y(1), at_y(3), to_zlo, to_core]
    barrier = pltpu.get_barrier_semaphore()
    for partner in partners:
        pl.semaphore_signal(barrier, inc=1, device_id=partner, device_id_type=MESH)

    copies = {}

    def send(name, src, dst, device):
        i = len(copies)
        assert i < N_SEM
        copy = pltpu.make_async_remote_copy(
            src_ref=src, dst_ref=dst, send_sem=send_sem.at[i], recv_sem=recv_sem.at[i],
            device_id=device, device_id_type=MESH,
        )
        copy.start()
        copies[name] = copy

    def recv(name):
        copies[name].wait_recv()

    local = []

    def fetch(src, dst):
        copy = pltpu.make_async_copy(src, dst, local_sem.at[len(local)])
        copy.start()
        local.append(copy)
        return copy

    piece = pl.multiple_of(core * 128 + y * 32, 32)
    own_cols = pl.ds(pl.multiple_of(x * SLAB, 128), SLAB)
    fetch_w = [
        fetch(wq, wraw.at[:, 0:256]),
        fetch(wk, wraw.at[:, 256:384]),
        fetch(wv, wraw.at[:, 384:512]),
    ]
    fetch_table = fetch(table_hbm, table)
    fetch_o = fetch(wo.at[pl.ds(piece, 32), own_cols], owslab.at[0, pl.ds(piece, 32), :])

    def column(row, k):
        n = 128 if k < 2 else 32
        return jnp.broadcast_to(gains[:, k * 128 : k * 128 + 128].T[0:n, row : row + 1], (n, 128))

    gain = jnp.concatenate([column(0, k) for k in range(3)], axis=0)
    for r in range(ROWS):
        block = hidden[r].astype(F32)
        xg[r, x, z] = (block * gain).astype(BF16)
        prex[0, r : r + 1, :] = jnp.sum(block * block, axis=0, keepdims=True)
    c_rows = jnp.concatenate([critique[0].astype(F32), jnp.zeros((12, WIDTH), F32)], axis=0)
    c_sums = jnp.sum(c_rows * c_rows, axis=-1, keepdims=True)
    prex[0, 4:8, :] = jnp.zeros((4, 128), F32)
    prex[0, 8:16, :] = jnp.broadcast_to(c_sums[0:8], (8, 128))
    c_rows = c_rows * gains[0:1, 0:WIDTH]
    c_last = jnp.concatenate([c_rows[:, 256:288], jnp.zeros((16, 96), F32)], axis=1)
    cg[0, 0] = jnp.concatenate([c_rows[:, 0:128], c_rows[:, 128:256], c_last], axis=0).astype(BF16)

    ssx[0] = jnp.zeros((24, 128), F32)
    pl.semaphore_wait(barrier, len(partners))

    zr, zl, zo = (z + 1) % 4, (z + 3) % 4, (z + 2) % 4
    xr, xl, xo = (x + 1) % 4, (x + 3) % 4, (x + 2) % 4
    main = pl.ds(0, FIRST)
    main_up, main_down = pl.ds(0, 128), pl.ds(128, FIRST - 128)
    rest = pl.ds(FIRST, WIDTH - FIRST)
    rest_up, rest_down = pl.ds(FIRST, 16), pl.ds(FIRST + 16, WIDTH - FIRST - 16)

    def pair_send(name, up, down, where):
        send(name + (0,), up, up, where(1))
        send(name + (1,), down, down, where(3))

    def z1(r):
        block = xg.at[r, x, z, main]
        pair_send(("z1", r), block, block, at_z)

    def x1(r, k, place):
        block = xg.at[r, x, place, main]
        pair_send(("x1", r, k), block, block, at_x)

    def x1a(r):
        x1(r, 0, z)

    def e1(r):
        recv(("z1", r, 0))
        recv(("z1", r, 1))
        pair_send(("z2", r), xg.at[r, x, zl, main_up], xg.at[r, x, zr, main_down], at_z)
        x1(r, 1, zl)
        x1(r, 3, zr)

    def e2(r):
        recv(("z2", r, 0))
        recv(("z2", r, 1))
        x1(r, 2, zo)

    def e3(r):
        for k in range(4):
            recv(("x1", r, k, 0))
            recv(("x1", r, k, 1))
        pair_send(("x2", r), xg.at[r, xl, :, main_up], xg.at[r, xr, :, main_down], at_x)

    def b1(r):
        block = xg.at[r, x, z, rest]
        pair_send(("b1", r), block, block, at_x)

    def b2(r):
        recv(("b1", r, 0))
        recv(("b1", r, 1))
        pair_send(("b2", r), xg.at[r, xl, z, rest_up], xg.at[r, xr, z, rest_down], at_x)

    def b3(r):
        recv(("b2", r, 0))
        recv(("b2", r, 1))
        block = xg.at[r, :, z, rest]
        pair_send(("b3", r), block, block, at_z)

    def b4(r):
        recv(("b3", r, 0))
        recv(("b3", r, 1))
        pair_send(("b4", r), xg.at[r, :, zl, rest_up], xg.at[r, :, zr, rest_down], at_z)

    def e4(r):
        for part in ("x2", "b4"):
            recv((part, r, 0))
            recv((part, r, 1))

    def ow_x():
        for d in (1, 3, 2):
            cols = pl.ds(pl.multiple_of(((x + d) % 4) * SLAB, 128), SLAB)
            send(("ow", d), wo.at[pl.ds(piece, 32), cols], owslab.at[4 - d, pl.ds(piece, 32), :], at_x(d))

    def ow_y1():
        fetch_o.wait()
        for d in (1, 3, 2):
            recv(("ow", d))
        here = owslab.at[:, pl.ds(piece, 32), :]
        send("owy1r", here, here, at_y(1))
        send("owy1l", here, here, at_y(3))

    def ow_y2():
        low = pl.ds(pl.multiple_of(core * 128 + ((y + 3) % 4) * 32, 32), 16)
        high = pl.ds(pl.multiple_of(core * 128 + ((y + 1) % 4) * 32 + 16, 16), 16)
        recv("owy1r")
        send("owy2r", owslab.at[:, low, :], owslab.at[:, low, :], at_y(1))
        recv("owy1l")
        send("owy2l", owslab.at[:, high, :], owslab.at[:, high, :], at_y(3))

    def ow_core():
        recv("owy2r")
        recv("owy2l")
        half = owslab.at[:, pl.ds(pl.multiple_of(core * 128, 128), 128), :]
        send("owc", half, half, to_core)

    def ow_turn():
        recv("owc")

        def step(d, carry):
            turned = owslab[d].T
            for zz in range(4):
                row = pl.multiple_of(((zz - z + 4) % 4) * WIDTH, 32)
                owt[d, pl.ds(row, WIDTH), :] = turned[zz * WIDTH : (zz + 1) * WIDTH]
            return carry

        lax.fori_loop(0, 4, step, 0)

    def gain_tables():
        for k in range(3):
            pgb[k * 128 : min(k * 128 + 128, WIDTH), :] = column(1, k)

    def rope_tables():
        fetch_table.wait()
        place = pl.multiple_of((s * 4 + y) * SPAN, SPAN)
        turned = table[pl.ds(place, SPAN), :].T
        cosT[...] = turned[0:64]
        sinT[...] = turned[64:128]

    def fetch_weights():
        for copy in fetch_w:
            copy.wait()

    def turn_weights(lo, hi):
        def step(c, carry):
            row = pl.multiple_of(c * 256, 256)
            wt[:, pl.ds(row, 256)] = wraw[pl.ds(row, 256), :].T
            return carry

        lax.fori_loop(lo, hi, step, 0)

    def pre_x():
        for d in (1, 3, 2):
            send(("px", d), prex.at[0], prex.at[4 - d], at_x(d))

    def pre_z():
        for d in (1, 3, 2):
            recv(("px", d))
        prez[0] = (prex[0] + prex[1]) + (prex[2] + prex[3])
        for d in (1, 3, 2):
            send(("pz", d), prez.at[0], prez.at[4 - d], at_z(d))

    def pre_done():
        for d in (1, 3, 2):
            recv(("pz", d))
        fac[...] = lax.rsqrt(((prez[0] + prez[1]) + (prez[2] + prez[3])) / D + EPS)

    def project(r):
        qkv = dot(wt[...], xg[r].reshape(D, SPAN)) * fac[r : r + 1, :]
        cosine, sine = cosT[...], sinT[...]

        def rotated(value):
            a, b = value[0:64], value[64:128]
            return jnp.concatenate([a * cosine - b * sine, b * cosine + a * sine], axis=0)

        qbuf[r, 0:128, :] = rotated(qkv[0:128]).T.astype(BF16)
        qbuf[r, 128:256, :] = rotated(qkv[128:256]).T.astype(BF16)
        kvg[r, 0, 0, 0, 0:128, :] = rotated(qkv[256:384]).astype(BF16)
        kvg[r, 0, 0, 0, 128:256, :] = qkv[384:512].astype(BF16)

    def kv_core(r, dy):
        send(("kvc", r, dy), kvg.at[r, 0, dy], kvg.at[r, 1, dy], to_core)

    def kv_y(name, r, dz):
        send((name, r, 0), kvg.at[r, 0, 0, dz], kvg.at[r, 0, 3, dz], at_y(1))
        send((name, r, 1), kvg.at[r, 0, 0, dz], kvg.at[r, 0, 1, dz], at_y(3))

    def kv_on(name, r, dz):
        send((name, r, 0), kvg.at[r, 0, 3, dz, 0:128], kvg.at[r, 0, 2, dz, 0:128], at_y(1))
        send((name, r, 1), kvg.at[r, 0, 1, dz, 128:256], kvg.at[r, 0, 2, dz, 128:256], at_y(3))

    def kva(r):
        send(("kvz", r), kvg.at[r, 0, 0, 0], kvg.at[r, 0, 0, 1], to_zlo)
        kv_y("kvy1", r, 0)

    def kvb(r):
        recv(("kvz", r))
        kv_y("kvy2", r, 1)
        kv_core(r, 0)

    def kvc(r):
        recv(("kvy1", r, 0))
        recv(("kvy1", r, 1))
        kv_on("kvy3", r, 0)

    def kvd(r):
        recv(("kvy2", r, 0))
        recv(("kvy2", r, 1))
        kv_on("kvy4", r, 1)
        kv_core(r, 1)
        kv_core(r, 3)

    def kve(r):
        for name in ("kvy3", "kvy4"):
            recv((name, r, 0))
            recv((name, r, 1))
        kv_core(r, 2)

    def key_start(b):
        dc, dy, dz = b // 8, (b // 2) % 4, b % 2
        section = ((zlo + dz) % 2) * 2 + (core + dc) % 2
        return (section * 4 + (y + dy) % 4) * SPAN

    def weigh(scores, keep):
        capped = CAP * jnp.tanh(scores * (SCALE / CAP))
        return jnp.where(keep, jnp.exp(capped), 0.0)

    def attend(r, j):
        if j == 0:
            for dy in range(4):
                recv(("kvc", r, dy))
        queries = qbuf[r, j * 128 : j * 128 + 128, :]
        length = lengths[r]
        token = (s * 4 + y) * SPAN + lax.broadcasted_iota(jnp.int32, (128, 128), 0)
        limit = jnp.minimum(token, length - 1)
        lane = lax.broadcasted_iota(jnp.int32, (128, 128), 1)

        def step(b, carry):
            num, den = carry
            for i in range(4):
                keys = kvg.at[r, b // 2, (b % 2) * 2 + i // 2, i % 2]
                weight = weigh(dot(queries, keys[0:128, :]), lane + key_start(b * 4 + i) <= limit)
                num = num + dot_t(weight.astype(BF16), keys[128:256, :])
                den = den + weight
            return num, den

        zero = jnp.zeros((128, 128), F32)
        num, den = lax.fori_loop(0, 4, step, (zero, zero))
        attg[r, 0, j] = (num / jnp.sum(den, axis=-1, keepdims=True)).astype(BF16)
        send(("ax1", r, j, 0), attg.at[r, 0, j], attg.at[r, 3, j], at_x(1))
        send(("ax1", r, j, 1), attg.at[r, 0, j], attg.at[r, 1, j], at_x(3))

    def ax2(r, j):
        recv(("ax1", r, j, 0))
        recv(("ax1", r, j, 1))
        send(("ax2", r, j, 0), attg.at[r, 3, j, 0:64], attg.at[r, 2, j, 0:64], at_x(1))
        send(("ax2", r, j, 1), attg.at[r, 1, j, 64:128], attg.at[r, 2, j, 64:128], at_x(3))

    low, high = pl.ds(0, HALF), pl.ds(HALF, HALF)

    def proj(r):
        for j in range(2):
            recv(("ax2", r, j, 0))
            recv(("ax2", r, j, 1))
        attended = [jnp.concatenate([attg[r, d, 0], attg[r, d, 1]], axis=1) for d in range(4)]
        for dz in (2, 1, 3, 0):
            rows = pl.ds(dz * WIDTH, WIDTH)
            part = dot_t(owt[0, rows, :], attended[0])
            for d in range(1, 4):
                part = part + dot_t(owt[d, rows, :], attended[d])
            if dz:
                pb[r, dz] = part.astype(BF16)
            else:
                own[r] = part
            if dz == 2:
                send(("rs1", r, 0), pb.at[r, 2, low], rs1.at[r, 0], at_z(1))
                send(("rs1", r, 1), pb.at[r, 2, high], rs1.at[r, 1], at_z(3))
            if dz == 1:
                send(("rs2", r, 0), pb.at[r, 1, high], rs2.at[r, 0, high], at_z(1))
            if dz == 3:
                send(("rs2", r, 1), pb.at[r, 3, low], rs2.at[r, 1, low], at_z(3))

    def rs_2(r):
        recv(("rs1", r, 0))
        pb[r, 1, 0:HALF] = (pb[r, 1, 0:HALF].astype(F32) + rs1[r, 0].astype(F32)).astype(BF16)
        send(("rs3", r, 0), pb.at[r, 1, low], rs2.at[r, 0, low], at_z(1))
        recv(("rs1", r, 1))
        pb[r, 3, HALF:WIDTH] = (pb[r, 3, HALF:WIDTH].astype(F32) + rs1[r, 1].astype(F32)).astype(BF16)
        send(("rs3", r, 1), pb.at[r, 3, high], rs2.at[r, 1, high], at_z(3))

    def rs_3(r):
        for name in ("rs2", "rs3"):
            recv((name, r, 0))
            recv((name, r, 1))
        share = own[r] + rs2[r, 0].astype(F32) + rs2[r, 1].astype(F32)
        own[r] = share
        ssx[0, r : r + 1, :] = jnp.sum(share * share, axis=0, keepdims=True)

    def c_x():
        for d in (1, 3, 2):
            send(("cx", d), cg.at[0, 0], cg.at[0, 4 - d], at_x(d))

    def c_z():
        for d in (1, 3, 2):
            recv(("cx", d))
        for d in (1, 3, 2):
            send(("cz", d), cg.at[0], cg.at[4 - d], at_z(d))

    lane8 = lax.broadcasted_iota(jnp.int32, (8, 128), 1)

    def c_project():
        for d in (1, 3, 2):
            recv(("cz", d))

        def step(dz, total):
            for dx in range(4):
                head = ((x + dx) % 4) * 4 + (z + dz) % 4
                row = pl.multiple_of(head * WIDTH, 32)
                total = total + dot(cg[dz, dx, 0:16], wraw[pl.ds(row, 128), :])
                total = total + dot(cg[dz, dx, 16:32], wraw[pl.ds(row + 128, 128), :])
                total = total + dot(cg[dz, dx, 32:48, 0:32], wraw[pl.ds(row + 256, 32), :])
            return total

        qkv = lax.fori_loop(0, 4, step, jnp.zeros((16, 512), F32))[0:8] * fac[8:16, 0:1]
        rest = jnp.zeros((8, 128), F32)
        angles = table[pl.ds(lengths[y], 8), :]
        other = pltpu.roll(angles, 64, 1)
        front = lane8 < 64
        cosine = jnp.where(front, angles, other)
        sine = jnp.where(front, -other, angles)

        def rotated(value):
            return value * cosine + pltpu.roll(value, 64, 1) * sine

        cq[...] = jnp.concatenate([rotated(qkv[:, 0:128]), rotated(qkv[:, 128:256])], axis=0).astype(BF16)
        ckv[0] = jnp.concatenate([rotated(qkv[:, 256:384]), rest], axis=0).astype(BF16)
        ckv[1] = jnp.concatenate([qkv[:, 384:512], rest], axis=0).astype(BF16)

    def c_attend():
        queries = cq[...]
        length = lengths[y]
        lane = lax.broadcasted_iota(jnp.int32, (16, 128), 1)

        num = jnp.zeros((16, 128), F32)
        den = jnp.zeros((16, 128), F32)
        for b in range(16):
            keys = kvg.at[y, b // 8, (b // 2) % 4, b % 2]
            weight = weigh(dot(queries, keys[0:128, :]), lane + key_start(b) < length)
            num = num + dot_t(weight.astype(BF16), keys[128:256, :])
            den = den + weight
        near = lax.broadcasted_iota(jnp.int32, (16, 16), 1) <= lax.broadcasted_iota(jnp.int32, (16, 16), 0) % 8
        weight = weigh(dot_t(queries, ckv[0]), near)
        num = num + dot(weight.astype(BF16), ckv[1])
        total = jnp.sum(den, axis=-1, keepdims=True) + jnp.sum(weight, axis=-1, keepdims=True)
        result = num / total
        rest = jnp.zeros((8, 128), F32)
        cattg[0, :, 0:128] = jnp.concatenate([result[0:8], rest], axis=0).astype(BF16)
        cattg[0, :, 128:256] = jnp.concatenate([result[8:16], rest], axis=0).astype(BF16)
        for d in (1, 3, 2):
            send(("ca", d), cattg.at[0], cattg.at[4 - d], at_x(d))

    def c_proj():
        for d in (1, 3, 2):
            recv(("ca", d))
        part = dot_t(cattg[0], owt[0])
        for d in range(1, 4):
            part = part + dot_t(cattg[d], owt[d])
        inside = lax.broadcasted_iota(jnp.int32, (16, 384), 1) < WIDTH
        for dz in range(4):
            moved = part if dz == 0 else pltpu.roll(part, SLAB - dz * WIDTH, 1)
            moved = jnp.where(inside, moved[:, 0:384], 0.0)
            if dz:
                cpj[dz] = moved.astype(BF16)
                send(("cr", dz), cpj.at[dz], crs.at[4 - dz], at_z(dz))
            else:
                cown[...] = moved

    def c_sum():
        share = cown[...]
        for d in (1, 3, 2):
            recv(("cr", d))
        for d in range(1, 4):
            share = share + crs[d].astype(F32)
        cown[...] = share
        ssx[0, 8:24, :] = jnp.broadcast_to(jnp.sum(share * share, axis=-1, keepdims=True), (16, 128))

    def sum_x():
        for d in (1, 3, 2):
            send(("sx", d), ssx.at[0], ssx.at[4 - d], at_x(d))

    def sum_z():
        for d in (1, 3, 2):
            recv(("sx", d))
        ssz[0] = (ssx[0] + ssx[1]) + (ssx[2] + ssx[3])
        for d in (1, 3, 2):
            send(("sz", d), ssz.at[0], ssz.at[4 - d], at_z(d))

    def finish():
        for d in (1, 3, 2):
            recv(("sz", d))
        factor = lax.rsqrt(((ssz[0] + ssz[1]) + (ssz[2] + ssz[3])) / D + EPS)
        for r in range(ROWS):
            part = own[r] * factor[r : r + 1, :] * pgb[...]
            out[r] = (hidden[r].astype(F32) + part).astype(BF16)
        for k in range(3):
            lo, hi = k * 128, min(k * 128 + 128, WIDTH)
            part = cown[0:4, k * 128 : k * 128 + 128] * factor[8:12, :] * gains[1:2, k * 128 : k * 128 + 128]
            c_out[0, :, lo:hi] = (critique[0, :, lo:hi].astype(F32) + part[:, 0 : hi - lo]).astype(BF16)

    z1(0)
    c_x()
    b1(0)
    x1a(0)
    b1(1)
    b1(3)
    pre_x()
    rope_tables()
    fetch_weights()
    turn_weights(0, 6)
    c_z()
    b2(0)
    x1a(1)
    ow_x()
    gain_tables()
    turn_weights(6, 12)
    turn_weights(12, 18)
    b2(1)
    b2(3)
    e1(0)
    b3(0)
    z1(2)
    pre_z()
    b1(2)
    z1(1)
    ow_y1()
    e2(0)
    x1a(2)
    b4(0)
    b2(2)
    e3(0)
    e1(2)
    b3(2)
    pre_done()
    c_project()
    ow_y2()
    e1(1)
    b3(1)
    z1(3)
    e4(0)
    project(0)
    kva(0)
    e2(2)
    ow_core()
    b4(2)
    kvc(0)
    e2(1)
    e3(2)
    x1a(3)
    kvb(0)
    b4(1)
    e3(1)
    kvd(0)
    e1(3)
    b3(3)
    kve(0)
    e4(2)
    project(2)
    kva(2)
    ow_turn()
    e2(3)
    attend(0, 0)
    e4(1)
    project(1)
    kvb(2)
    kvc(2)
    attend(0, 1)
    kva(1)
    b4(3)
    e3(3)
    ax2(0, 0)
    kvd(2)
    ax2(0, 1)
    kvb(1)
    kvc(1)
    kve(2)
    e4(3)
    project(3)
    kvd(1)
    kva(3)
    attend(2, 0)
    attend(2, 1)
    kve(1)
    proj(0)
    ax2(2, 0)
    kvb(3)
    kvc(3)
    attend(1, 0)
    ax2(2, 1)
    attend(1, 1)
    rs_2(0)
    kvd(3)
    ax2(1, 0)
    proj(2)
    ax2(1, 1)
    kve(3)
    rs_3(0)
    proj(1)
    attend(3, 0)
    rs_2(2)
    attend(3, 1)
    c_attend()
    ax2(3, 0)
    rs_2(1)
    ax2(3, 1)
    c_proj()
    proj(3)
    rs_3(2)
    rs_3(1)
    c_sum()
    rs_2(3)
    rs_3(3)
    sum_x()
    sum_z()
    finish()
    for copy in copies.values():
        copy.wait_send()


def body(hidden, critique, lengths, pre_gain, post_gain, q_weight, k_weight, v_weight, o_weight):
    own_gain = lax.dynamic_slice(pre_gain, (lax.axis_index("head") * WIDTH,), (WIDTH,))
    gains = jnp.pad(jnp.stack([own_gain, post_gain]).astype(F32), ((0, 6), (0, 384 - WIDTH)))
    table = jnp.asarray(rope_table())
    vmem = pl.BlockSpec(memory_space=pltpu.VMEM)
    smem = pl.BlockSpec(memory_space=pltpu.SMEM)
    anywhere = pl.BlockSpec(memory_space=pl.ANY)
    turned = jnp.transpose(hidden, (0, 2, 1))
    result, c_result = pl.pallas_call(
        kernel,
        out_shape=(
            jax.ShapeDtypeStruct(turned.shape, BF16),
            jax.ShapeDtypeStruct(critique.shape, BF16),
        ),
        in_specs=[vmem, vmem, smem, vmem, anywhere, anywhere, anywhere, anywhere, anywhere],
        out_specs=(vmem, vmem),
        scratch_shapes=[
            pltpu.VMEM((ROWS, 4, 4, WIDTH, SPAN), BF16),
            pltpu.VMEM((D, 512), BF16),
            pltpu.VMEM((512, D), BF16),
            pltpu.VMEM((WIDTH, 128), F32),
            pltpu.VMEM((2056, 128), F32),
            pltpu.VMEM((64, SPAN), F32),
            pltpu.VMEM((64, SPAN), F32),
            pltpu.VMEM((ROWS, 256, HEAD), BF16),
            pltpu.VMEM((ROWS, 2, 4, 2, 256, SPAN), BF16),
            pltpu.VMEM((ROWS, 4, 2, SPAN, HEAD), BF16),
            pltpu.VMEM((4, 256, SLAB), BF16),
            pltpu.VMEM((4, SLAB, 256), BF16),
            pltpu.VMEM((ROWS, 4, WIDTH, SPAN), BF16),
            pltpu.VMEM((ROWS, WIDTH, SPAN), F32),
            pltpu.VMEM((ROWS, 2, HALF, SPAN), BF16),
            pltpu.VMEM((ROWS, 2, WIDTH, SPAN), BF16),
            pltpu.VMEM((4, 4, 48, 128), BF16),
            pltpu.VMEM((16, 128), BF16),
            pltpu.VMEM((2, 16, 128), BF16),
            pltpu.VMEM((4, 16, 256), BF16),
            pltpu.VMEM((4, 16, 384), BF16),
            pltpu.VMEM((16, 384), F32),
            pltpu.VMEM((4, 16, 384), BF16),
            pltpu.VMEM((4, 24, 128), F32),
            pltpu.VMEM((4, 24, 128), F32),
            pltpu.VMEM((4, 16, 128), F32),
            pltpu.VMEM((4, 16, 128), F32),
            pltpu.VMEM((16, 128), F32),
            pltpu.SemaphoreType.DMA((N_SEM,)),
            pltpu.SemaphoreType.DMA((N_SEM,)),
            pltpu.SemaphoreType.DMA((8,)),
        ],
        compiler_params=pltpu.CompilerParams(
            collective_id=0, has_side_effects=True, vmem_limit_bytes=56 * 1024 * 1024
        ),
        cost_estimate=pl.CostEstimate(flops=5_000_000_000, bytes_accessed=16_000_000, transcendentals=4_000_000),
    )(turned, critique, lengths, gains, table, q_weight, k_weight, v_weight, o_weight)
    return jnp.transpose(result, (0, 2, 1)), c_result


def solution(mesh):
    return jax.shard_map(
        body,
        mesh=mesh,
        in_specs=(
            P(None, ("section", "seq"), "head"),
            P("seq", None, "head"),
            P(),
            P(),
            P("head"),
            P(None, "head"),
            P(None, "head"),
            P(None, "head"),
            P("head", None),
        ),
        out_specs=(P(None, ("section", "seq"), "head"), P("seq", None, "head")),
        check_vma=False,
    )
```

```python
import math

import jax
import jax.numpy as jnp
import numpy as np
from jax import lax
from jax.experimental import pallas as pl
from jax.experimental.pallas import tpu as pltpu
from jax.sharding import PartitionSpec as P

D = 4608
HEADS = 32
KV_HEADS = 16
HEAD = 128
ROWS = 4
SPAN = 128
WIDTH = 288
SLAB = 4 * WIDTH
HALF = WIDTH // 2
STEPS = 4

EPS = 1e-06
CAP = 50.0
BASE = 10000.0
SCALE = (D // HEADS) ** (-0.5)
F32 = jnp.float32
BF16 = jnp.bfloat16
MESH = pl.DeviceIdType.MESH
N_SEM = 184


def rope_table():
    freq = np.exp(np.arange(64, dtype=np.float64) * (-2.0 * math.log(BASE) / HEAD))
    angle = np.arange(2056, dtype=np.float64)[:, None] * freq
    return np.concatenate([np.cos(angle), np.sin(angle)], axis=-1).astype(np.float32)


def dot(a, b):
    return jnp.dot(a, b, preferred_element_type=F32)


def dot_t(a, b):
    return lax.dot_general(a, b, (((1,), (1,)), ((), ())), preferred_element_type=F32)


def kernel(
    hidden, critique, lengths, gains, table_hbm, wq, wk, wv, wo,
    out, c_out,
    xg, wraw, wt, pgb, table, cosT, sinT, qbuf, kvg, attg, owslab, owt,
    pb, own, rs1, rs2, cg, cq, ckv, cattg, cpj, cown, crs, ssx, ssz, prex, prez, fac,
    send_sem, recv_sem, local_sem,
):
    s = lax.axis_index("section")
    y = lax.axis_index("seq")
    h = lax.axis_index("head")
    x, z = h // 4, h % 4
    zlo, core = s // 2, s % 2

    def at_x(d):
        return {"head": ((x + d) % 4) * 4 + z}

    def at_z(d):
        return {"head": x * 4 + (z + d) % 4}

    def at_y(d):
        return {"seq": (y + d) % 4}

    to_zlo = {"section": (1 - zlo) * 2 + core}
    to_core = {"section": zlo * 2 + 1 - core}

    partners = [at_x(1), at_x(3), at_x(2), at_z(1), at_z(3), at_z(2), at_y(1), at_y(3), to_zlo, to_core]
    barrier = pltpu.get_barrier_semaphore()
    for partner in partners:
        pl.semaphore_signal(barrier, inc=1, device_id=partner, device_id_type=MESH)

    copies = {}

    def send(name, src, dst, device):
        i = len(copies)
        assert i < N_SEM
        copy = pltpu.make_async_remote_copy(
            src_ref=src, dst_ref=dst, send_sem=send_sem.at[i], recv_sem=recv_sem.at[i],
            device_id=device, device_id_type=MESH,
        )
        copy.start()
        copies[name] = copy

    def recv(name):
        copies[name].wait_recv()

    local = []

    def fetch(src, dst):
        copy = pltpu.make_async_copy(src, dst, local_sem.at[len(local)])
        copy.start()
        local.append(copy)
        return copy

    piece = pl.multiple_of(core * 128 + y * 32, 32)
    own_cols = pl.ds(pl.multiple_of(x * SLAB, 128), SLAB)
    fetch_w = [
        fetch(wq, wraw.at[:, 0:256]),
        fetch(wk, wraw.at[:, 256:384]),
        fetch(wv, wraw.at[:, 384:512]),
    ]
    fetch_table = fetch(table_hbm, table)
    fetch_o = fetch(wo.at[pl.ds(piece, 32), own_cols], owslab.at[0, pl.ds(piece, 32), :])

    def column(row, k):
        n = 128 if k < 2 else 32
        return jnp.broadcast_to(gains[:, k * 128 : k * 128 + 128].T[0:n, row : row + 1], (n, 128))

    gain = jnp.concatenate([column(0, k) for k in range(3)], axis=0)
    for r in range(ROWS):
        block = hidden[r].astype(F32)
        xg[r, x, z] = (block * gain).astype(BF16)
        prex[0, r : r + 1, :] = jnp.sum(block * block, axis=0, keepdims=True)
    c_rows = jnp.concatenate([critique[0].astype(F32), jnp.zeros((12, WIDTH), F32)], axis=0)
    c_sums = jnp.sum(c_rows * c_rows, axis=-1, keepdims=True)
    prex[0, 4:8, :] = jnp.zeros((4, 128), F32)
    prex[0, 8:16, :] = jnp.broadcast_to(c_sums[0:8], (8, 128))
    c_rows = c_rows * gains[0:1, 0:WIDTH]
    c_last = jnp.concatenate([c_rows[:, 256:288], jnp.zeros((16, 96), F32)], axis=1)
    cg[0, 0] = jnp.concatenate([c_rows[:, 0:128], c_rows[:, 128:256], c_last], axis=0).astype(BF16)

    ssx[0] = jnp.zeros((24, 128), F32)
    pl.semaphore_wait(barrier, len(partners))

    zr, zl, zo = (z + 1) % 4, (z + 3) % 4, (z + 2) % 4
    xr, xl, xo = (x + 1) % 4, (x + 3) % 4, (x + 2) % 4
    main = pl.ds(0, WIDTH)
    main_up, main_down = pl.ds(0, HALF), pl.ds(HALF, HALF)

    def pair_send(name, up, down, where):
        send(name + (0,), up, up, where(1))
        send(name + (1,), down, down, where(3))

    def z1(r):
        block = xg.at[r, x, z, main]
        pair_send(("z1", r), block, block, at_z)

    def x1(r, k, place):
        block = xg.at[r, x, place, main]
        pair_send(("x1", r, k), block, block, at_x)

    def x1a(r):
        x1(r, 0, z)

    def e1(r):
        recv(("z1", r, 0))
        recv(("z1", r, 1))
        pair_send(("z2", r), xg.at[r, x, zl, main_up], xg.at[r, x, zr, main_down], at_z)
        x1(r, 1, zl)
        x1(r, 3, zr)

    def e2(r):
        recv(("z2", r, 0))
        recv(("z2", r, 1))
        x1(r, 2, zo)

    def e3(r):
        for k in range(4):
            recv(("x1", r, k, 0))
            recv(("x1", r, k, 1))
        pair_send(("x2", r), xg.at[r, xl, :, main_up], xg.at[r, xr, :, main_down], at_x)

    def e4(r):
        recv(("x2", r, 0))
        recv(("x2", r, 1))

    def ow_x():
        for d in (1, 3, 2):
            cols = pl.ds(pl.multiple_of(((x + d) % 4) * SLAB, 128), SLAB)
            send(("ow", d), wo.at[pl.ds(piece, 32), cols], owslab.at[4 - d, pl.ds(piece, 32), :], at_x(d))

    def ow_y1():
        fetch_o.wait()
        for d in (1, 3, 2):
            recv(("ow", d))
        here = owslab.at[:, pl.ds(piece, 32), :]
        send("owy1r", here, here, at_y(1))
        send("owy1l", here, here, at_y(3))

    def ow_y2():
        low = pl.ds(pl.multiple_of(core * 128 + ((y + 3) % 4) * 32, 32), 16)
        high = pl.ds(pl.multiple_of(core * 128 + ((y + 1) % 4) * 32 + 16, 16), 16)
        recv("owy1r")
        send("owy2r", owslab.at[:, low, :], owslab.at[:, low, :], at_y(1))
        recv("owy1l")
        send("owy2l", owslab.at[:, high, :], owslab.at[:, high, :], at_y(3))

    def ow_core():
        recv("owy2r")
        recv("owy2l")
        half = owslab.at[:, pl.ds(pl.multiple_of(core * 128, 128), 128), :]
        send("owc", half, half, to_core)

    def ow_turn():
        recv("owc")

        def step(d, carry):
            turned = owslab[d].T
            for zz in range(4):
                row = pl.multiple_of(((zz - z + 4) % 4) * WIDTH, 32)
                owt[d, pl.ds(row, WIDTH), :] = turned[zz * WIDTH : (zz + 1) * WIDTH]
            return carry

        lax.fori_loop(0, 4, step, 0)

    def gain_tables():
        for k in range(3):
            pgb[k * 128 : min(k * 128 + 128, WIDTH), :] = column(1, k)

    def rope_tables():
        fetch_table.wait()
        place = pl.multiple_of((s * 4 + y) * SPAN, SPAN)
        turned = table[pl.ds(place, SPAN), :].T
        cosT[...] = turned[0:64]
        sinT[...] = turned[64:128]

    def fetch_weights():
        for copy in fetch_w:
            copy.wait()

    def turn_weights(lo, hi):
        def step(c, carry):
            row = pl.multiple_of(c * 256, 256)
            wt[:, pl.ds(row, 256)] = wraw[pl.ds(row, 256), :].T
            return carry

        lax.fori_loop(lo, hi, step, 0)

    def pre_x():
        for d in (1, 3, 2):
            send(("px", d), prex.at[0], prex.at[4 - d], at_x(d))

    def pre_z():
        for d in (1, 3, 2):
            recv(("px", d))
        prez[0] = (prex[0] + prex[1]) + (prex[2] + prex[3])
        for d in (1, 3, 2):
            send(("pz", d), prez.at[0], prez.at[4 - d], at_z(d))

    def pre_done():
        for d in (1, 3, 2):
            recv(("pz", d))
        fac[...] = lax.rsqrt(((prez[0] + prez[1]) + (prez[2] + prez[3])) / D + EPS)

    def project(r):
        qkv = dot(wt[...], xg[r].reshape(D, SPAN)) * fac[r : r + 1, :]
        cosine, sine = cosT[...], sinT[...]

        def rotated(value):
            a, b = value[0:64], value[64:128]
            return jnp.concatenate([a * cosine - b * sine, b * cosine + a * sine], axis=0)

        qbuf[r, 0:128, :] = rotated(qkv[0:128]).T.astype(BF16)
        qbuf[r, 128:256, :] = rotated(qkv[128:256]).T.astype(BF16)
        kvg[r, 0, 0, 0, 0:128, :] = rotated(qkv[256:384]).astype(BF16)
        kvg[r, 0, 0, 0, 128:256, :] = qkv[384:512].astype(BF16)

    def kv_core(r, dy):
        send(("kvc", r, dy), kvg.at[r, 0, dy], kvg.at[r, 1, dy], to_core)

    def kv_y(name, r, dz):
        send((name, r, 0), kvg.at[r, 0, 0, dz], kvg.at[r, 0, 3, dz], at_y(1))
        send((name, r, 1), kvg.at[r, 0, 0, dz], kvg.at[r, 0, 1, dz], at_y(3))

    def kv_on(name, r, dz):
        send((name, r, 0), kvg.at[r, 0, 3, dz, 0:128], kvg.at[r, 0, 2, dz, 0:128], at_y(1))
        send((name, r, 1), kvg.at[r, 0, 1, dz, 128:256], kvg.at[r, 0, 2, dz, 128:256], at_y(3))

    def kva(r):
        send(("kvz", r), kvg.at[r, 0, 0, 0], kvg.at[r, 0, 0, 1], to_zlo)
        kv_y("kvy1", r, 0)

    def kvb(r):
        recv(("kvz", r))
        kv_y("kvy2", r, 1)
        kv_core(r, 0)

    def kvc(r):
        recv(("kvy1", r, 0))
        recv(("kvy1", r, 1))
        kv_on("kvy3", r, 0)

    def kvd(r):
        recv(("kvy2", r, 0))
        recv(("kvy2", r, 1))
        kv_on("kvy4", r, 1)
        kv_core(r, 1)
        kv_core(r, 3)

    def kve(r):
        for name in ("kvy3", "kvy4"):
            recv((name, r, 0))
            recv((name, r, 1))
        kv_core(r, 2)

    def key_start(b):
        dc, dy, dz = b // 8, (b // 2) % 4, b % 2
        section = ((zlo + dz) % 2) * 2 + (core + dc) % 2
        return (section * 4 + (y + dy) % 4) * SPAN

    def weigh(scores, keep):
        return jnp.where(keep, jnp.exp2(jnp.tanh(scores * (SCALE / CAP)) * (CAP * math.log2(math.e))), 0.0)

    def attend(r):
        for dy in range(4):
            recv(("kvc", r, dy))
        queries = qbuf[r]
        length = lengths[r]
        token = (s * 4 + y) * SPAN + lax.broadcasted_iota(jnp.int32, (256, 128), 0) % SPAN
        limit = jnp.minimum(token, length - 1)
        lane = lax.broadcasted_iota(jnp.int32, (256, 128), 1)

        num = jnp.zeros((256, 128), F32)
        den = jnp.zeros((256, 128), F32)
        for i in range(16):
            keys = kvg.at[r, i // 8, (i // 2) % 4, i % 2]
            weight = weigh(dot(queries, keys[0:128, :]), lane + key_start(i) <= limit)
            num = num + dot_t(weight.astype(BF16), keys[128:256, :])
            den = den + weight
        result = num / jnp.sum(den, axis=-1, keepdims=True)
        for k in range(2):
            attg[r, 0, k] = result[k * 128 : k * 128 + 128].astype(BF16)
        send(("ax1", r, 0), attg.at[r, 0], attg.at[r, 3], at_x(1))
        send(("ax1", r, 1), attg.at[r, 0], attg.at[r, 1], at_x(3))

    def ax2(r):
        recv(("ax1", r, 0))
        recv(("ax1", r, 1))
        send(("ax2", r, 0), attg.at[r, 3, 0], attg.at[r, 2, 0], at_x(1))
        send(("ax2", r, 1), attg.at[r, 1, 1], attg.at[r, 2, 1], at_x(3))

    low, high = pl.ds(0, HALF), pl.ds(HALF, HALF)

    def proj(r):
        recv(("ax2", r, 0))
        recv(("ax2", r, 1))
        attended = [jnp.concatenate([attg[r, d, 0], attg[r, d, 1]], axis=1) for d in range(4)]
        for dz in (2, 1, 3, 0):
            rows = pl.ds(dz * WIDTH, WIDTH)
            part = dot_t(owt[0, rows, :], attended[0])
            for d in range(1, 4):
                part = part + dot_t(owt[d, rows, :], attended[d])
            if dz:
                pb[r, dz] = part.astype(BF16)
            else:
                own[r] = part
            if dz == 2:
                send(("rs1", r, 0), pb.at[r, 2, low], rs1.at[r, 0], at_z(1))
                send(("rs1", r, 1), pb.at[r, 2, high], rs1.at[r, 1], at_z(3))
            if dz == 1:
                send(("rs2", r, 0), pb.at[r, 1, high], rs2.at[r, 0, high], at_z(1))
            if dz == 3:
                send(("rs2", r, 1), pb.at[r, 3, low], rs2.at[r, 1, low], at_z(3))

    def rs_2(r):
        recv(("rs1", r, 0))
        pb[r, 1, 0:HALF] = (pb[r, 1, 0:HALF].astype(F32) + rs1[r, 0].astype(F32)).astype(BF16)
        send(("rs3", r, 0), pb.at[r, 1, low], rs2.at[r, 0, low], at_z(1))
        recv(("rs1", r, 1))
        pb[r, 3, HALF:WIDTH] = (pb[r, 3, HALF:WIDTH].astype(F32) + rs1[r, 1].astype(F32)).astype(BF16)
        send(("rs3", r, 1), pb.at[r, 3, high], rs2.at[r, 1, high], at_z(3))

    def rs_3(r):
        for name in ("rs2", "rs3"):
            recv((name, r, 0))
            recv((name, r, 1))
        share = own[r] + rs2[r, 0].astype(F32) + rs2[r, 1].astype(F32)
        own[r] = share
        ssx[0, r : r + 1, :] = jnp.sum(share * share, axis=0, keepdims=True)

    def c_x():
        for d in (1, 3, 2):
            send(("cx", d), cg.at[0, 0], cg.at[0, 4 - d], at_x(d))

    def c_z():
        for d in (1, 3, 2):
            recv(("cx", d))
        for d in (1, 3, 2):
            send(("cz", d), cg.at[0], cg.at[4 - d], at_z(d))

    lane8 = lax.broadcasted_iota(jnp.int32, (8, 128), 1)

    def c_project():
        for d in (1, 3, 2):
            recv(("cz", d))

        def step(dz, total):
            for dx in range(4):
                head = ((x + dx) % 4) * 4 + (z + dz) % 4
                row = pl.multiple_of(head * WIDTH, 32)
                total = total + dot(cg[dz, dx, 0:16], wraw[pl.ds(row, 128), :])
                total = total + dot(cg[dz, dx, 16:32], wraw[pl.ds(row + 128, 128), :])
                total = total + dot(cg[dz, dx, 32:48, 0:32], wraw[pl.ds(row + 256, 32), :])
            return total

        qkv = lax.fori_loop(0, 4, step, jnp.zeros((16, 512), F32))[0:8] * fac[8:16, 0:1]
        rest = jnp.zeros((8, 128), F32)
        angles = table[pl.ds(lengths[y], 8), :]
        other = pltpu.roll(angles, 64, 1)
        front = lane8 < 64
        cosine = jnp.where(front, angles, other)
        sine = jnp.where(front, -other, angles)

        def rotated(value):
            return value * cosine + pltpu.roll(value, 64, 1) * sine

        cq[...] = jnp.concatenate([rotated(qkv[:, 0:128]), rotated(qkv[:, 128:256])], axis=0).astype(BF16)
        ckv[0] = jnp.concatenate([rotated(qkv[:, 256:384]), rest], axis=0).astype(BF16)
        ckv[1] = jnp.concatenate([qkv[:, 384:512], rest], axis=0).astype(BF16)

    def c_attend():
        queries = cq[...]
        length = lengths[y]
        lane = lax.broadcasted_iota(jnp.int32, (16, 128), 1)

        num = jnp.zeros((16, 128), F32)
        den = jnp.zeros((16, 128), F32)
        for b in range(16):
            keys = kvg.at[y, b // 8, (b // 2) % 4, b % 2]
            weight = weigh(dot(queries, keys[0:128, :]), lane + key_start(b) < length)
            num = num + dot_t(weight.astype(BF16), keys[128:256, :])
            den = den + weight
        near = lax.broadcasted_iota(jnp.int32, (16, 16), 1) <= lax.broadcasted_iota(jnp.int32, (16, 16), 0) % 8
        weight = weigh(dot_t(queries, ckv[0]), near)
        num = num + dot(weight.astype(BF16), ckv[1])
        total = jnp.sum(den, axis=-1, keepdims=True) + jnp.sum(weight, axis=-1, keepdims=True)
        result = num / total
        rest = jnp.zeros((8, 128), F32)
        cattg[0, :, 0:128] = jnp.concatenate([result[0:8], rest], axis=0).astype(BF16)
        cattg[0, :, 128:256] = jnp.concatenate([result[8:16], rest], axis=0).astype(BF16)
        for d in (1, 3, 2):
            send(("ca", d), cattg.at[0], cattg.at[4 - d], at_x(d))

    def c_proj():
        for d in (1, 3, 2):
            recv(("ca", d))
        part = dot_t(cattg[0], owt[0])
        for d in range(1, 4):
            part = part + dot_t(cattg[d], owt[d])
        inside = lax.broadcasted_iota(jnp.int32, (16, 384), 1) < WIDTH
        for dz in range(4):
            moved = part if dz == 0 else pltpu.roll(part, SLAB - dz * WIDTH, 1)
            moved = jnp.where(inside, moved[:, 0:384], 0.0)
            if dz:
                cpj[dz] = moved.astype(BF16)
                send(("cr", dz), cpj.at[dz], crs.at[4 - dz], at_z(dz))
            else:
                cown[...] = moved

    def c_sum():
        share = cown[...]
        for d in (1, 3, 2):
            recv(("cr", d))
        for d in range(1, 4):
            share = share + crs[d].astype(F32)
        cown[...] = share
        ssx[0, 8:24, :] = jnp.broadcast_to(jnp.sum(share * share, axis=-1, keepdims=True), (16, 128))

    def sum_x():
        for d in (1, 3, 2):
            send(("sx", d), ssx.at[0], ssx.at[4 - d], at_x(d))

    def sum_z():
        for d in (1, 3, 2):
            recv(("sx", d))
        ssz[0] = (ssx[0] + ssx[1]) + (ssx[2] + ssx[3])
        for d in (1, 3, 2):
            send(("sz", d), ssz.at[0], ssz.at[4 - d], at_z(d))

    def finish():
        for d in (1, 3, 2):
            recv(("sz", d))
        factor = lax.rsqrt(((ssz[0] + ssz[1]) + (ssz[2] + ssz[3])) / D + EPS)
        for r in range(ROWS):
            part = own[r] * factor[r : r + 1, :] * pgb[...]
            out[r] = (hidden[r].astype(F32) + part).astype(BF16)
        for k in range(3):
            lo, hi = k * 128, min(k * 128 + 128, WIDTH)
            part = cown[0:4, k * 128 : k * 128 + 128] * factor[8:12, :] * gains[1:2, k * 128 : k * 128 + 128]
            c_out[0, :, lo:hi] = (critique[0, :, lo:hi].astype(F32) + part[:, 0 : hi - lo]).astype(BF16)

    x1a(0)
    pre_x()
    x1a(1)
    ow_x()
    fetch_weights()
    turn_weights(0, 6)
    turn_weights(6, 12)
    rope_tables()
    c_x()
    gain_tables()
    z1(0)
    turn_weights(12, 18)
    pre_z()
    z1(1)
    e1(0)
    z1(2)
    pre_done()
    ow_y1()
    c_z()
    e1(1)
    z1(3)
    e2(0)
    x1a(2)
    e1(2)
    ow_y2()
    e3(0)
    ow_core()
    c_project()
    e2(1)
    x1a(3)
    e4(0)
    project(0)
    kva(0)
    e1(3)
    e3(1)
    e2(2)
    ow_turn()
    kvc(0)
    kvb(0)
    e2(3)
    kvd(0)
    e4(1)
    project(1)
    kve(0)
    kva(1)
    e3(2)
    attend(0)
    e3(3)
    kvc(1)
    kvb(1)
    e4(2)
    project(2)
    kva(2)
    ax2(0)
    kvd(1)
    kvc(2)
    kvb(2)
    e4(3)
    project(3)
    kve(1)
    kva(3)
    proj(0)
    kvd(2)
    attend(1)
    kvc(3)
    kvb(3)
    kve(2)
    rs_2(0)
    ax2(1)
    attend(2)
    kvd(3)
    rs_3(0)
    proj(1)
    kve(3)
    ax2(2)
    attend(3)
    rs_2(1)
    c_attend()
    proj(2)
    ax2(3)
    c_proj()
    rs_3(1)
    proj(3)
    rs_2(2)
    c_sum()
    rs_2(3)
    rs_3(2)
    rs_3(3)
    sum_x()
    sum_z()
    finish()
    for copy in copies.values():
        copy.wait_send()


def body(hidden, critique, lengths, pre_gain, post_gain, q_weight, k_weight, v_weight, o_weight):
    own_gain = lax.dynamic_slice(pre_gain, (lax.axis_index("head") * WIDTH,), (WIDTH,))
    gains = jnp.pad(jnp.stack([own_gain, post_gain]).astype(F32), ((0, 6), (0, 384 - WIDTH)))
    table = jnp.asarray(rope_table())
    vmem = pl.BlockSpec(memory_space=pltpu.VMEM)
    smem = pl.BlockSpec(memory_space=pltpu.SMEM)
    anywhere = pl.BlockSpec(memory_space=pl.ANY)
    turned = jnp.transpose(hidden, (0, 2, 1))
    result, c_result = pl.pallas_call(
        kernel,
        out_shape=(
            jax.ShapeDtypeStruct(turned.shape, BF16),
            jax.ShapeDtypeStruct(critique.shape, BF16),
        ),
        in_specs=[vmem, vmem, smem, vmem, anywhere, anywhere, anywhere, anywhere, anywhere],
        out_specs=(vmem, vmem),
        scratch_shapes=[
            pltpu.VMEM((ROWS, 4, 4, WIDTH, SPAN), BF16),
            pltpu.VMEM((D, 512), BF16),
            pltpu.VMEM((512, D), BF16),
            pltpu.VMEM((WIDTH, 128), F32),
            pltpu.VMEM((2056, 128), F32),
            pltpu.VMEM((64, SPAN), F32),
            pltpu.VMEM((64, SPAN), F32),
            pltpu.VMEM((ROWS, 256, HEAD), BF16),
            pltpu.VMEM((ROWS, 2, 4, 2, 256, SPAN), BF16),
            pltpu.VMEM((ROWS, 4, 2, SPAN, HEAD), BF16),
            pltpu.VMEM((4, 256, SLAB), BF16),
            pltpu.VMEM((4, SLAB, 256), BF16),
            pltpu.VMEM((ROWS, 4, WIDTH, SPAN), BF16),
            pltpu.VMEM((ROWS, WIDTH, SPAN), F32),
            pltpu.VMEM((ROWS, 2, HALF, SPAN), BF16),
            pltpu.VMEM((ROWS, 2, WIDTH, SPAN), BF16),
            pltpu.VMEM((4, 4, 48, 128), BF16),
            pltpu.VMEM((16, 128), BF16),
            pltpu.VMEM((2, 16, 128), BF16),
            pltpu.VMEM((4, 16, 256), BF16),
            pltpu.VMEM((4, 16, 384), BF16),
            pltpu.VMEM((16, 384), F32),
            pltpu.VMEM((4, 16, 384), BF16),
            pltpu.VMEM((4, 24, 128), F32),
            pltpu.VMEM((4, 24, 128), F32),
            pltpu.VMEM((4, 16, 128), F32),
            pltpu.VMEM((4, 16, 128), F32),
            pltpu.VMEM((16, 128), F32),
            pltpu.SemaphoreType.DMA((N_SEM,)),
            pltpu.SemaphoreType.DMA((N_SEM,)),
            pltpu.SemaphoreType.DMA((8,)),
        ],
        compiler_params=pltpu.CompilerParams(
            collective_id=0, has_side_effects=True, vmem_limit_bytes=56 * 1024 * 1024
        ),
        cost_estimate=pl.CostEstimate(flops=5_000_000_000, bytes_accessed=16_000_000, transcendentals=4_000_000),
    )(turned, critique, lengths, gains, table, q_weight, k_weight, v_weight, o_weight)
    return jnp.transpose(result, (0, 2, 1)), c_result


def solution(mesh):
    return jax.shard_map(
        body,
        mesh=mesh,
        in_specs=(
            P(None, ("section", "seq"), "head"),
            P("seq", None, "head"),
            P(),
            P(),
            P("head"),
            P(None, "head"),
            P(None, "head"),
            P(None, "head"),
            P("head", None),
        ),
        out_specs=(P(None, ("section", "seq"), "head"), P("seq", None, "head")),
        check_vma=False,
    )
```

```python
import math

import jax
import jax.numpy as jnp
import numpy as np
from jax import lax
from jax.experimental import pallas as pl
from jax.experimental.pallas import tpu as pltpu
from jax.sharding import PartitionSpec as P

D = 4608
HEADS = 32
KV_HEADS = 16
HEAD = 128
ROWS = 4
SPAN = 128
WIDTH = 288
SLAB = 4 * WIDTH
HALF = WIDTH // 2
STEPS = 4

EPS = 1e-06
CAP = 50.0
BASE = 10000.0
SCALE = (D // HEADS) ** (-0.5)
F32 = jnp.float32
BF16 = jnp.bfloat16
MESH = pl.DeviceIdType.MESH
N_SEM = 184


def rope_table():
    freq = np.exp(np.arange(64, dtype=np.float64) * (-2.0 * math.log(BASE) / HEAD))
    angle = np.arange(2056, dtype=np.float64)[:, None] * freq
    return np.concatenate([np.cos(angle), np.sin(angle)], axis=-1).astype(np.float32)


def dot(a, b):
    return jnp.dot(a, b, preferred_element_type=F32)


def dot_t(a, b):
    return lax.dot_general(a, b, (((1,), (1,)), ((), ())), preferred_element_type=F32)


def kernel(
    hidden, critique, lengths, gains, table_hbm, wq, wk, wv, wo,
    out, c_out,
    xg, wraw, wt, pgb, table, cosT, sinT, qbuf, kvg, attg, owslab, owt,
    pb, own, rs1, rs2, cg, cq, ckv, cattg, cpj, cown, crs, ssx, ssz, prex, prez, fac,
    send_sem, recv_sem, local_sem,
):
    s = lax.axis_index("section")
    y = lax.axis_index("seq")
    h = lax.axis_index("head")
    x, z = h // 4, h % 4
    zlo, core = s // 2, s % 2

    def at_x(d):
        return {"head": ((x + d) % 4) * 4 + z}

    def at_z(d):
        return {"head": x * 4 + (z + d) % 4}

    def at_y(d):
        return {"seq": (y + d) % 4}

    to_zlo = {"section": (1 - zlo) * 2 + core}
    to_core = {"section": zlo * 2 + 1 - core}

    partners = [at_x(1), at_x(3), at_x(2), at_z(1), at_z(3), at_z(2), at_y(1), at_y(3), to_zlo, to_core]
    barrier = pltpu.get_barrier_semaphore()
    for partner in partners:
        pl.semaphore_signal(barrier, inc=1, device_id=partner, device_id_type=MESH)

    copies = {}

    def send(name, src, dst, device):
        i = len(copies)
        assert i < N_SEM
        copy = pltpu.make_async_remote_copy(
            src_ref=src, dst_ref=dst, send_sem=send_sem.at[i], recv_sem=recv_sem.at[i],
            device_id=device, device_id_type=MESH,
        )
        copy.start()
        copies[name] = copy

    def recv(name):
        copies[name].wait_recv()

    local = []

    def fetch(src, dst):
        copy = pltpu.make_async_copy(src, dst, local_sem.at[len(local)])
        copy.start()
        local.append(copy)
        return copy

    piece = pl.multiple_of(core * 128 + y * 32, 32)
    own_cols = pl.ds(pl.multiple_of(x * SLAB, 128), SLAB)
    fetch_w = [
        fetch(wq, wraw.at[:, 0:256]),
        fetch(wk, wraw.at[:, 256:384]),
        fetch(wv, wraw.at[:, 384:512]),
    ]
    fetch_table = fetch(table_hbm, table)
    fetch_o = fetch(wo.at[pl.ds(piece, 32), own_cols], owslab.at[0, pl.ds(piece, 32), :])

    def column(row, k):
        n = 128 if k < 2 else 32
        return jnp.broadcast_to(gains[:, k * 128 : k * 128 + 128].T[0:n, row : row + 1], (n, 128))

    gain = jnp.concatenate([column(0, k) for k in range(3)], axis=0)
    for r in range(ROWS):
        block = hidden[r].astype(F32)
        xg[r, x, z] = (block * gain).astype(BF16)
        prex[0, r : r + 1, :] = jnp.sum(block * block, axis=0, keepdims=True)
    c_rows = jnp.concatenate([critique[0].astype(F32), jnp.zeros((12, WIDTH), F32)], axis=0)
    c_sums = jnp.sum(c_rows * c_rows, axis=-1, keepdims=True)
    prex[0, 4:8, :] = jnp.zeros((4, 128), F32)
    prex[0, 8:16, :] = jnp.broadcast_to(c_sums[0:8], (8, 128))
    c_rows = c_rows * gains[0:1, 0:WIDTH]
    c_last = jnp.concatenate([c_rows[:, 256:288], jnp.zeros((16, 96), F32)], axis=1)
    cg[0, 0] = jnp.concatenate([c_rows[:, 0:128], c_rows[:, 128:256], c_last], axis=0).astype(BF16)

    ssx[0] = jnp.zeros((24, 128), F32)
    pl.semaphore_wait(barrier, len(partners))

    zr, zl, zo = (z + 1) % 4, (z + 3) % 4, (z + 2) % 4
    xr, xl, xo = (x + 1) % 4, (x + 3) % 4, (x + 2) % 4
    main = pl.ds(0, WIDTH)
    main_up, main_down = pl.ds(0, HALF), pl.ds(HALF, HALF)

    def pair_send(name, up, down, where):
        send(name + (0,), up, up, where(1))
        send(name + (1,), down, down, where(3))

    def z1(r):
        block = xg.at[r, x, z, main]
        pair_send(("z1", r), block, block, at_z)

    def x1(r, k, place):
        block = xg.at[r, x, place, main]
        pair_send(("x1", r, k), block, block, at_x)

    def x1a(r):
        x1(r, 0, z)

    def e1(r):
        recv(("z1", r, 0))
        recv(("z1", r, 1))
        pair_send(("z2", r), xg.at[r, x, zl, main_up], xg.at[r, x, zr, main_down], at_z)
        x1(r, 1, zl)
        x1(r, 3, zr)

    def e2(r):
        recv(("z2", r, 0))
        recv(("z2", r, 1))
        x1(r, 2, zo)

    def e3(r):
        for k in range(4):
            recv(("x1", r, k, 0))
            recv(("x1", r, k, 1))
        pair_send(("x2", r), xg.at[r, xl, :, main_up], xg.at[r, xr, :, main_down], at_x)

    def e4(r):
        recv(("x2", r, 0))
        recv(("x2", r, 1))

    def ow_x():
        for d in (1, 3, 2):
            cols = pl.ds(pl.multiple_of(((x + d) % 4) * SLAB, 128), SLAB)
            send(("ow", d), wo.at[pl.ds(piece, 32), cols], owslab.at[4 - d, pl.ds(piece, 32), :], at_x(d))

    def ow_y1():
        fetch_o.wait()
        for d in (1, 3, 2):
            recv(("ow", d))
        here = owslab.at[:, pl.ds(piece, 32), :]
        send("owy1r", here, here, at_y(1))
        send("owy1l", here, here, at_y(3))

    def ow_y2():
        low = pl.ds(pl.multiple_of(core * 128 + ((y + 3) % 4) * 32, 32), 16)
        high = pl.ds(pl.multiple_of(core * 128 + ((y + 1) % 4) * 32 + 16, 16), 16)
        recv("owy1r")
        send("owy2r", owslab.at[:, low, :], owslab.at[:, low, :], at_y(1))
        recv("owy1l")
        send("owy2l", owslab.at[:, high, :], owslab.at[:, high, :], at_y(3))

    def ow_core():
        recv("owy2r")
        recv("owy2l")
        half = owslab.at[:, pl.ds(pl.multiple_of(core * 128, 128), 128), :]
        send("owc", half, half, to_core)

    def ow_turn():
        recv("owc")

        def step(d, carry):
            turned = owslab[d].T
            for zz in range(4):
                row = pl.multiple_of(((zz - z + 4) % 4) * WIDTH, 32)
                owt[d, pl.ds(row, WIDTH), :] = turned[zz * WIDTH : (zz + 1) * WIDTH]
            return carry

        lax.fori_loop(0, 4, step, 0)

    def gain_tables():
        for k in range(3):
            pgb[k * 128 : min(k * 128 + 128, WIDTH), :] = column(1, k)

    def rope_tables():
        fetch_table.wait()
        place = pl.multiple_of((s * 4 + y) * SPAN, SPAN)
        turned = table[pl.ds(place, SPAN), :].T
        cosT[...] = turned[0:64]
        sinT[...] = turned[64:128]

    def fetch_weights():
        for copy in fetch_w:
            copy.wait()

    def turn_weights(lo, hi):
        def step(c, carry):
            row = pl.multiple_of(c * 256, 256)
            wt[:, pl.ds(row, 256)] = wraw[pl.ds(row, 256), :].T
            return carry

        lax.fori_loop(lo, hi, step, 0)

    def pre_x():
        for d in (1, 3, 2):
            send(("px", d), prex.at[0], prex.at[4 - d], at_x(d))

    def pre_z():
        for d in (1, 3, 2):
            recv(("px", d))
        prez[0] = (prex[0] + prex[1]) + (prex[2] + prex[3])
        for d in (1, 3, 2):
            send(("pz", d), prez.at[0], prez.at[4 - d], at_z(d))

    def pre_done():
        for d in (1, 3, 2):
            recv(("pz", d))
        fac[...] = lax.rsqrt(((prez[0] + prez[1]) + (prez[2] + prez[3])) / D + EPS)

    def project(r):
        qkv = dot(wt[...], xg[r].reshape(D, SPAN)) * fac[r : r + 1, :]
        cosine, sine = cosT[...], sinT[...]

        def rotated(value):
            a, b = value[0:64], value[64:128]
            return jnp.concatenate([a * cosine - b * sine, b * cosine + a * sine], axis=0)

        qbuf[r, 0:128, :] = rotated(qkv[0:128]).T.astype(BF16)
        qbuf[r, 128:256, :] = rotated(qkv[128:256]).T.astype(BF16)
        kvg[r, 0, 0, 0, 0:128, :] = rotated(qkv[256:384]).astype(BF16)
        kvg[r, 0, 0, 0, 128:256, :] = qkv[384:512].astype(BF16)

    def kv_core(r, dy):
        send(("kvc", r, dy), kvg.at[r, 0, dy], kvg.at[r, 1, dy], to_core)

    def kv_y(name, r, dz):
        send((name, r, 0), kvg.at[r, 0, 0, dz], kvg.at[r, 0, 3, dz], at_y(1))
        send((name, r, 1), kvg.at[r, 0, 0, dz], kvg.at[r, 0, 1, dz], at_y(3))

    def kv_on(name, r, dz):
        send((name, r, 0), kvg.at[r, 0, 3, dz, 0:128], kvg.at[r, 0, 2, dz, 0:128], at_y(1))
        send((name, r, 1), kvg.at[r, 0, 1, dz, 128:256], kvg.at[r, 0, 2, dz, 128:256], at_y(3))

    def kva(r):
        send(("kvz", r), kvg.at[r, 0, 0, 0], kvg.at[r, 0, 0, 1], to_zlo)
        kv_y("kvy1", r, 0)

    def kvb(r):
        recv(("kvz", r))
        kv_y("kvy2", r, 1)
        kv_core(r, 0)

    def kvc(r):
        recv(("kvy1", r, 0))
        recv(("kvy1", r, 1))
        kv_on("kvy3", r, 0)

    def kvd(r):
        recv(("kvy2", r, 0))
        recv(("kvy2", r, 1))
        kv_on("kvy4", r, 1)
        kv_core(r, 1)
        kv_core(r, 3)

    def kve(r):
        for name in ("kvy3", "kvy4"):
            recv((name, r, 0))
            recv((name, r, 1))
        kv_core(r, 2)

    def key_start(b):
        dc, dy, dz = b // 8, (b // 2) % 4, b % 2
        section = ((zlo + dz) % 2) * 2 + (core + dc) % 2
        return (section * 4 + (y + dy) % 4) * SPAN

    def weigh(scores, keep):
        return jnp.where(keep, jnp.exp2(jnp.tanh(scores * (SCALE / CAP)) * (CAP * math.log2(math.e))), 0.0)

    def attend(r):
        for dy in range(4):
            recv(("kvc", r, dy))
        queries = qbuf[r]
        length = lengths[r]
        token = (s * 4 + y) * SPAN + lax.broadcasted_iota(jnp.int32, (256, 128), 0) % SPAN
        limit = jnp.minimum(token, length - 1)
        lane = lax.broadcasted_iota(jnp.int32, (256, 128), 1)

        num = jnp.zeros((256, 128), F32)
        den = jnp.zeros((256, 128), F32)
        for i in range(16):
            keys = kvg.at[r, i // 8, (i // 2) % 4, i % 2]
            weight = weigh(dot(queries, keys[0:128, :]), lane + key_start(i) <= limit)
            num = num + dot_t(weight.astype(BF16), keys[128:256, :])
            den = den + weight
        result = num / jnp.sum(den, axis=-1, keepdims=True)
        for k in range(2):
            attg[r, 0, k] = result[k * 128 : k * 128 + 128].astype(BF16)
        send(("ax1", r, 0), attg.at[r, 0], attg.at[r, 3], at_x(1))
        send(("ax1", r, 1), attg.at[r, 0], attg.at[r, 1], at_x(3))

    def ax2(r):
        recv(("ax1", r, 0))
        recv(("ax1", r, 1))
        send(("ax2", r, 0), attg.at[r, 3, 0], attg.at[r, 2, 0], at_x(1))
        send(("ax2", r, 1), attg.at[r, 1, 1], attg.at[r, 2, 1], at_x(3))

    low, high = pl.ds(0, HALF), pl.ds(HALF, HALF)

    def proj(r):
        recv(("ax2", r, 0))
        recv(("ax2", r, 1))
        attended = [jnp.concatenate([attg[r, d, 0], attg[r, d, 1]], axis=1) for d in range(4)]
        for dz in (2, 1, 3, 0):
            rows = pl.ds(dz * WIDTH, WIDTH)
            part = dot_t(owt[0, rows, :], attended[0])
            for d in range(1, 4):
                part = part + dot_t(owt[d, rows, :], attended[d])
            if dz:
                pb[r, dz] = part.astype(BF16)
            else:
                own[r] = part
            if dz == 2:
                send(("rs1", r, 0), pb.at[r, 2, low], rs1.at[r, 0], at_z(1))
                send(("rs1", r, 1), pb.at[r, 2, high], rs1.at[r, 1], at_z(3))
            if dz == 1:
                send(("rs2", r, 0), pb.at[r, 1, high], rs2.at[r, 0, high], at_z(1))
            if dz == 3:
                send(("rs2", r, 1), pb.at[r, 3, low], rs2.at[r, 1, low], at_z(3))

    def rs_2(r):
        recv(("rs1", r, 0))
        pb[r, 1, 0:HALF] = (pb[r, 1, 0:HALF].astype(F32) + rs1[r, 0].astype(F32)).astype(BF16)
        send(("rs3", r, 0), pb.at[r, 1, low], rs2.at[r, 0, low], at_z(1))
        recv(("rs1", r, 1))
        pb[r, 3, HALF:WIDTH] = (pb[r, 3, HALF:WIDTH].astype(F32) + rs1[r, 1].astype(F32)).astype(BF16)
        send(("rs3", r, 1), pb.at[r, 3, high], rs2.at[r, 1, high], at_z(3))

    def rs_3(r):
        for name in ("rs2", "rs3"):
            recv((name, r, 0))
            recv((name, r, 1))
        share = own[r] + rs2[r, 0].astype(F32) + rs2[r, 1].astype(F32)
        own[r] = share
        ssx[0, r : r + 1, :] = jnp.sum(share * share, axis=0, keepdims=True)

    def c_x():
        for d in (1, 3, 2):
            send(("cx", d), cg.at[0, 0], cg.at[0, 4 - d], at_x(d))

    def c_z():
        for d in (1, 3, 2):
            recv(("cx", d))
        for d in (1, 3, 2):
            send(("cz", d), cg.at[0], cg.at[4 - d], at_z(d))

    lane8 = lax.broadcasted_iota(jnp.int32, (8, 128), 1)

    def c_project():
        for d in (1, 3, 2):
            recv(("cz", d))

        def step(dz, total):
            for dx in range(4):
                head = ((x + dx) % 4) * 4 + (z + dz) % 4
                row = pl.multiple_of(head * WIDTH, 32)
                total = total + dot(cg[dz, dx, 0:16], wraw[pl.ds(row, 128), :])
                total = total + dot(cg[dz, dx, 16:32], wraw[pl.ds(row + 128, 128), :])
                total = total + dot(cg[dz, dx, 32:48, 0:32], wraw[pl.ds(row + 256, 32), :])
            return total

        qkv = lax.fori_loop(0, 4, step, jnp.zeros((16, 512), F32))[0:8] * fac[8:16, 0:1]
        rest = jnp.zeros((8, 128), F32)
        angles = table[pl.ds(lengths[y], 8), :]
        other = pltpu.roll(angles, 64, 1)
        front = lane8 < 64
        cosine = jnp.where(front, angles, other)
        sine = jnp.where(front, -other, angles)

        def rotated(value):
            return value * cosine + pltpu.roll(value, 64, 1) * sine

        cq[...] = jnp.concatenate([rotated(qkv[:, 0:128]), rotated(qkv[:, 128:256])], axis=0).astype(BF16)
        ckv[0] = jnp.concatenate([rotated(qkv[:, 256:384]), rest], axis=0).astype(BF16)
        ckv[1] = jnp.concatenate([qkv[:, 384:512], rest], axis=0).astype(BF16)

    def c_attend():
        queries = cq[...]
        length = lengths[y]
        lane = lax.broadcasted_iota(jnp.int32, (16, 128), 1)

        num = jnp.zeros((16, 128), F32)
        den = jnp.zeros((16, 128), F32)
        for b in range(16):
            keys = kvg.at[y, b // 8, (b // 2) % 4, b % 2]
            weight = weigh(dot(queries, keys[0:128, :]), lane + key_start(b) < length)
            num = num + dot_t(weight.astype(BF16), keys[128:256, :])
            den = den + weight
        near = lax.broadcasted_iota(jnp.int32, (16, 16), 1) <= lax.broadcasted_iota(jnp.int32, (16, 16), 0) % 8
        weight = weigh(dot_t(queries, ckv[0]), near)
        num = num + dot(weight.astype(BF16), ckv[1])
        total = jnp.sum(den, axis=-1, keepdims=True) + jnp.sum(weight, axis=-1, keepdims=True)
        result = num / total
        rest = jnp.zeros((8, 128), F32)
        cattg[0, :, 0:128] = jnp.concatenate([result[0:8], rest], axis=0).astype(BF16)
        cattg[0, :, 128:256] = jnp.concatenate([result[8:16], rest], axis=0).astype(BF16)
        for d in (1, 3, 2):
            send(("ca", d), cattg.at[0], cattg.at[4 - d], at_x(d))

    def c_proj():
        for d in (1, 3, 2):
            recv(("ca", d))
        part = dot_t(cattg[0], owt[0])
        for d in range(1, 4):
            part = part + dot_t(cattg[d], owt[d])
        inside = lax.broadcasted_iota(jnp.int32, (16, 384), 1) < WIDTH
        for dz in range(4):
            moved = part if dz == 0 else pltpu.roll(part, SLAB - dz * WIDTH, 1)
            moved = jnp.where(inside, moved[:, 0:384], 0.0)
            if dz:
                cpj[dz] = moved.astype(BF16)
                send(("cr", dz), cpj.at[dz], crs.at[4 - dz], at_z(dz))
            else:
                cown[...] = moved

    def c_sum():
        share = cown[...]
        for d in (1, 3, 2):
            recv(("cr", d))
        for d in range(1, 4):
            share = share + crs[d].astype(F32)
        cown[...] = share
        ssx[0, 8:24, :] = jnp.broadcast_to(jnp.sum(share * share, axis=-1, keepdims=True), (16, 128))

    def sum_x():
        for d in (1, 3, 2):
            send(("sx", d), ssx.at[0], ssx.at[4 - d], at_x(d))

    def sum_z():
        for d in (1, 3, 2):
            recv(("sx", d))
        ssz[0] = (ssx[0] + ssx[1]) + (ssx[2] + ssx[3])
        for d in (1, 3, 2):
            send(("sz", d), ssz.at[0], ssz.at[4 - d], at_z(d))

    def finish():
        for d in (1, 3, 2):
            recv(("sz", d))
        factor = lax.rsqrt(((ssz[0] + ssz[1]) + (ssz[2] + ssz[3])) / D + EPS)
        for r in range(ROWS):
            part = own[r] * factor[r : r + 1, :] * pgb[...]
            out[r] = (hidden[r].astype(F32) + part).astype(BF16)
        for k in range(3):
            lo, hi = k * 128, min(k * 128 + 128, WIDTH)
            part = cown[0:4, k * 128 : k * 128 + 128] * factor[8:12, :] * gains[1:2, k * 128 : k * 128 + 128]
            c_out[0, :, lo:hi] = (critique[0, :, lo:hi].astype(F32) + part[:, 0 : hi - lo]).astype(BF16)

    x1a(1)
    z1(0)
    x1a(0)
    c_x()
    ow_x()
    fetch_weights()
    turn_weights(0, 6)
    pre_x()
    turn_weights(6, 12)
    turn_weights(12, 18)
    z1(1)
    rope_tables()
    gain_tables()
    e1(0)
    c_z()
    z1(2)
    e1(1)
    z1(3)
    e2(0)
    ow_y1()
    x1a(2)
    pre_z()
    ow_y2()
    e3(0)
    e1(2)
    e2(1)
    x1a(3)
    ow_core()
    e4(0)
    e1(3)
    pre_done()
    project(0)
    c_project()
    kva(0)
    e3(1)
    e2(2)
    e2(3)
    ow_turn()
    kvc(0)
    kvb(0)
    kvd(0)
    e4(1)
    project(1)
    kve(0)
    kva(1)
    e3(2)
    attend(0)
    kvc(1)
    e3(3)
    kvb(1)
    e4(2)
    project(2)
    kva(2)
    ax2(0)
    kvd(1)
    kvc(2)
    kvb(2)
    e4(3)
    project(3)
    kva(3)
    kve(1)
    proj(0)
    kvd(2)
    attend(1)
    kvc(3)
    kvb(3)
    kve(2)
    rs_2(0)
    ax2(1)
    attend(2)
    kvd(3)
    rs_3(0)
    proj(1)
    kve(3)
    ax2(2)
    attend(3)
    rs_2(1)
    c_attend()
    proj(2)
    ax2(3)
    c_proj()
    rs_3(1)
    proj(3)
    rs_2(2)
    c_sum()
    rs_2(3)
    rs_3(2)
    rs_3(3)
    sum_x()
    sum_z()
    finish()
    for copy in copies.values():
        copy.wait_send()


def hand_over(result, c_result, out, c_out):
    out[...] = result[...]
    c_out[...] = c_result[...]


def body(hidden, critique, lengths, pre_gain, post_gain, q_weight, k_weight, v_weight, o_weight):
    own_gain = lax.dynamic_slice(pre_gain, (lax.axis_index("head") * WIDTH,), (WIDTH,))
    gains = jnp.pad(jnp.stack([own_gain, post_gain]).astype(F32), ((0, 6), (0, 384 - WIDTH)))
    table = jnp.asarray(rope_table())
    vmem = pl.BlockSpec(memory_space=pltpu.VMEM)
    smem = pl.BlockSpec(memory_space=pltpu.SMEM)
    anywhere = pl.BlockSpec(memory_space=pl.ANY)
    turned = jnp.transpose(hidden, (0, 2, 1))
    result, c_result = pl.pallas_call(
        kernel,
        out_shape=(
            jax.ShapeDtypeStruct(turned.shape, BF16),
            jax.ShapeDtypeStruct(critique.shape, BF16),
        ),
        in_specs=[vmem, vmem, smem, vmem, anywhere, anywhere, anywhere, anywhere, anywhere],
        out_specs=(vmem, vmem),
        scratch_shapes=[
            pltpu.VMEM((ROWS, 4, 4, WIDTH, SPAN), BF16),
            pltpu.VMEM((D, 512), BF16),
            pltpu.VMEM((512, D), BF16),
            pltpu.VMEM((WIDTH, 128), F32),
            pltpu.VMEM((2056, 128), F32),
            pltpu.VMEM((64, SPAN), F32),
            pltpu.VMEM((64, SPAN), F32),
            pltpu.VMEM((ROWS, 256, HEAD), BF16),
            pltpu.VMEM((ROWS, 2, 4, 2, 256, SPAN), BF16),
            pltpu.VMEM((ROWS, 4, 2, SPAN, HEAD), BF16),
            pltpu.VMEM((4, 256, SLAB), BF16),
            pltpu.VMEM((4, SLAB, 256), BF16),
            pltpu.VMEM((ROWS, 4, WIDTH, SPAN), BF16),
            pltpu.VMEM((ROWS, WIDTH, SPAN), F32),
            pltpu.VMEM((ROWS, 2, HALF, SPAN), BF16),
            pltpu.VMEM((ROWS, 2, WIDTH, SPAN), BF16),
            pltpu.VMEM((4, 4, 48, 128), BF16),
            pltpu.VMEM((16, 128), BF16),
            pltpu.VMEM((2, 16, 128), BF16),
            pltpu.VMEM((4, 16, 256), BF16),
            pltpu.VMEM((4, 16, 384), BF16),
            pltpu.VMEM((16, 384), F32),
            pltpu.VMEM((4, 16, 384), BF16),
            pltpu.VMEM((4, 24, 128), F32),
            pltpu.VMEM((4, 24, 128), F32),
            pltpu.VMEM((4, 16, 128), F32),
            pltpu.VMEM((4, 16, 128), F32),
            pltpu.VMEM((16, 128), F32),
            pltpu.SemaphoreType.DMA((N_SEM,)),
            pltpu.SemaphoreType.DMA((N_SEM,)),
            pltpu.SemaphoreType.DMA((8,)),
        ],
        compiler_params=pltpu.CompilerParams(
            collective_id=0, has_side_effects=True, vmem_limit_bytes=56 * 1024 * 1024
        ),
        cost_estimate=pl.CostEstimate(flops=5_000_000_000, bytes_accessed=16_000_000, transcendentals=4_000_000),
    )(turned, critique, lengths, gains, table, q_weight, k_weight, v_weight, o_weight)
    result, c_result = pl.pallas_call(
        hand_over,
        out_shape=(
            jax.ShapeDtypeStruct(turned.shape, BF16),
            jax.ShapeDtypeStruct(critique.shape, BF16),
        ),
        in_specs=[vmem, vmem],
        out_specs=(vmem, vmem),
    )(result, c_result)
    return jnp.transpose(result, (0, 2, 1)), c_result


def solution(mesh):
    return jax.shard_map(
        body,
        mesh=mesh,
        in_specs=(
            P(None, ("section", "seq"), "head"),
            P("seq", None, "head"),
            P(),
            P(),
            P("head"),
            P(None, "head"),
            P(None, "head"),
            P(None, "head"),
            P("head", None),
        ),
        out_specs=(P(None, ("section", "seq"), "head"), P("seq", None, "head")),
        check_vma=False,
    )
```

```python
import math

import jax
import jax.numpy as jnp
import numpy as np
from jax import lax
from jax.experimental import pallas as pl
from jax.experimental.pallas import tpu as pltpu
from jax.sharding import PartitionSpec as P

D = 4608
HEADS = 32
KV_HEADS = 16
HEAD = 128
ROWS = 4
SPAN = 128
WIDTH = 288
SLAB = 4 * WIDTH
HALF = WIDTH // 2
STEPS = 4

EPS = 1e-06
CAP = 50.0
BASE = 10000.0
SCALE = (D // HEADS) ** (-0.5)
F32 = jnp.float32
BF16 = jnp.bfloat16
MESH = pl.DeviceIdType.MESH
N_SEM = 184


def rope_table():
    freq = np.exp(np.arange(64, dtype=np.float64) * (-2.0 * math.log(BASE) / HEAD))
    angle = np.arange(2056, dtype=np.float64)[:, None] * freq
    return np.concatenate([np.cos(angle), np.sin(angle)], axis=-1).astype(np.float32)


def dot(a, b):
    return jnp.dot(a, b, preferred_element_type=F32)


def dot_t(a, b):
    return lax.dot_general(a, b, (((1,), (1,)), ((), ())), preferred_element_type=F32)


def kernel(
    hidden, critique, lengths, pre_gain, post_gain, table_hbm, wq, wk, wv, wo,
    out, c_out,
    xg, wraw, wt, pgb, table, cosT, sinT, qbuf, kvg, attg, owslab, owt,
    pb, own, rs1, rs2, cg, cq, ckv, cattg, cpj, cown, crs, ssx, ssz, prex, prez, fac, gains,
    send_sem, recv_sem, local_sem,
):
    s = lax.axis_index("section")
    y = lax.axis_index("seq")
    h = lax.axis_index("head")
    x, z = h // 4, h % 4
    zlo, core = s // 2, s % 2

    def at_x(d):
        return {"head": ((x + d) % 4) * 4 + z}

    def at_z(d):
        return {"head": x * 4 + (z + d) % 4}

    def at_y(d):
        return {"seq": (y + d) % 4}

    to_zlo = {"section": (1 - zlo) * 2 + core}
    to_core = {"section": zlo * 2 + 1 - core}

    partners = [at_x(1), at_x(3), at_x(2), at_z(1), at_z(3), at_z(2), at_y(1), at_y(3), to_zlo, to_core]
    barrier = pltpu.get_barrier_semaphore()
    for partner in partners:
        pl.semaphore_signal(barrier, inc=1, device_id=partner, device_id_type=MESH)

    copies = {}

    def send(name, src, dst, device):
        i = len(copies)
        assert i < N_SEM
        copy = pltpu.make_async_remote_copy(
            src_ref=src, dst_ref=dst, send_sem=send_sem.at[i], recv_sem=recv_sem.at[i],
            device_id=device, device_id_type=MESH,
        )
        copy.start()
        copies[name] = copy

    def recv(name):
        copies[name].wait_recv()

    local = []

    def fetch(src, dst):
        copy = pltpu.make_async_copy(src, dst, local_sem.at[len(local)])
        copy.start()
        local.append(copy)
        return copy

    piece = pl.multiple_of(core * 128 + y * 32, 32)
    own_cols = pl.ds(pl.multiple_of(x * SLAB, 128), SLAB)
    fetch_w = [
        fetch(wq, wraw.at[:, 0:256]),
        fetch(wk, wraw.at[:, 256:384]),
        fetch(wv, wraw.at[:, 384:512]),
    ]
    fetch_table = fetch(table_hbm, table)
    fetch_o = fetch(wo.at[pl.ds(piece, 32), own_cols], owslab.at[0, pl.ds(piece, 32), :])

    mine = lax.broadcasted_iota(jnp.int32, (16, WIDTH), 0) == h
    own_gain = jnp.sum(jnp.where(mine, pre_gain[...].astype(F32), 0.0), axis=0, keepdims=True)
    gains[...] = jnp.zeros((8, 384), F32)
    gains[0:1, 0:WIDTH] = own_gain
    gains[1:2, 0:WIDTH] = post_gain[...].astype(F32)

    def column(row, k):
        n = 128 if k < 2 else 32
        return jnp.broadcast_to(gains[:, k * 128 : k * 128 + 128].T[0:n, row : row + 1], (n, 128))

    gain = jnp.concatenate([column(0, k) for k in range(3)], axis=0)
    for r in range(ROWS):
        block = hidden[r].astype(F32)
        xg[r, x, z] = (block * gain).astype(BF16)
        prex[0, r : r + 1, :] = jnp.sum(block * block, axis=0, keepdims=True)
    c_rows = jnp.concatenate([critique[0].astype(F32), jnp.zeros((12, WIDTH), F32)], axis=0)
    c_sums = jnp.sum(c_rows * c_rows, axis=-1, keepdims=True)
    prex[0, 4:8, :] = jnp.zeros((4, 128), F32)
    prex[0, 8:16, :] = jnp.broadcast_to(c_sums[0:8], (8, 128))
    c_rows = c_rows * gains[0:1, 0:WIDTH]
    c_last = jnp.concatenate([c_rows[:, 256:288], jnp.zeros((16, 96), F32)], axis=1)
    cg[0, 0] = jnp.concatenate([c_rows[:, 0:128], c_rows[:, 128:256], c_last], axis=0).astype(BF16)

    ssx[0] = jnp.zeros((24, 128), F32)
    pl.semaphore_wait(barrier, len(partners))

    zr, zl, zo = (z + 1) % 4, (z + 3) % 4, (z + 2) % 4
    xr, xl, xo = (x + 1) % 4, (x + 3) % 4, (x + 2) % 4
    main = pl.ds(0, WIDTH)
    main_up, main_down = pl.ds(0, HALF), pl.ds(HALF, HALF)

    def pair_send(name, up, down, where):
        send(name + (0,), up, up, where(1))
        send(name + (1,), down, down, where(3))

    def z1(r):
        block = xg.at[r, x, z, main]
        pair_send(("z1", r), block, block, at_z)

    def x1(r, k, place):
        block = xg.at[r, x, place, main]
        pair_send(("x1", r, k), block, block, at_x)

    def x1a(r):
        x1(r, 0, z)

    def e1(r):
        recv(("z1", r, 0))
        recv(("z1", r, 1))
        pair_send(("z2", r), xg.at[r, x, zl, main_up], xg.at[r, x, zr, main_down], at_z)
        x1(r, 1, zl)
        x1(r, 3, zr)

    def e2(r):
        recv(("z2", r, 0))
        recv(("z2", r, 1))
        x1(r, 2, zo)

    def e3(r):
        for k in range(4):
            recv(("x1", r, k, 0))
            recv(("x1", r, k, 1))
        pair_send(("x2", r), xg.at[r, xl, :, main_up], xg.at[r, xr, :, main_down], at_x)

    def e4(r):
        recv(("x2", r, 0))
        recv(("x2", r, 1))

    def ow_x():
        for d in (1, 3, 2):
            cols = pl.ds(pl.multiple_of(((x + d) % 4) * SLAB, 128), SLAB)
            send(("ow", d), wo.at[pl.ds(piece, 32), cols], owslab.at[4 - d, pl.ds(piece, 32), :], at_x(d))

    def ow_y1():
        fetch_o.wait()
        for d in (1, 3, 2):
            recv(("ow", d))
        here = owslab.at[:, pl.ds(piece, 32), :]
        send("owy1r", here, here, at_y(1))
        send("owy1l", here, here, at_y(3))

    def ow_y2():
        low = pl.ds(pl.multiple_of(core * 128 + ((y + 3) % 4) * 32, 32), 16)
        high = pl.ds(pl.multiple_of(core * 128 + ((y + 1) % 4) * 32 + 16, 16), 16)
        recv("owy1r")
        send("owy2r", owslab.at[:, low, :], owslab.at[:, low, :], at_y(1))
        recv("owy1l")
        send("owy2l", owslab.at[:, high, :], owslab.at[:, high, :], at_y(3))

    def ow_core():
        recv("owy2r")
        recv("owy2l")
        half = owslab.at[:, pl.ds(pl.multiple_of(core * 128, 128), 128), :]
        send("owc", half, half, to_core)

    def ow_turn():
        recv("owc")

        def step(d, carry):
            turned = owslab[d].T
            for zz in range(4):
                row = pl.multiple_of(((zz - z + 4) % 4) * WIDTH, 32)
                owt[d, pl.ds(row, WIDTH), :] = turned[zz * WIDTH : (zz + 1) * WIDTH]
            return carry

        lax.fori_loop(0, 4, step, 0)

    def gain_tables():
        for k in range(3):
            pgb[k * 128 : min(k * 128 + 128, WIDTH), :] = column(1, k)

    def rope_tables():
        fetch_table.wait()
        place = pl.multiple_of((s * 4 + y) * SPAN, SPAN)
        turned = table[pl.ds(place, SPAN), :].T
        cosT[...] = turned[0:64]
        sinT[...] = turned[64:128]

    def fetch_weights():
        for copy in fetch_w:
            copy.wait()

    def turn_weights(lo, hi):
        def step(c, carry):
            row = pl.multiple_of(c * 256, 256)
            wt[:, pl.ds(row, 256)] = wraw[pl.ds(row, 256), :].T
            return carry

        lax.fori_loop(lo, hi, step, 0)

    def pre_x():
        for d in (1, 3, 2):
            send(("px", d), prex.at[0], prex.at[4 - d], at_x(d))

    def pre_z():
        for d in (1, 3, 2):
            recv(("px", d))
        prez[0] = (prex[0] + prex[1]) + (prex[2] + prex[3])
        for d in (1, 3, 2):
            send(("pz", d), prez.at[0], prez.at[4 - d], at_z(d))

    def pre_done():
        for d in (1, 3, 2):
            recv(("pz", d))
        fac[...] = lax.rsqrt(((prez[0] + prez[1]) + (prez[2] + prez[3])) / D + EPS)

    def project(r):
        qkv = dot(wt[...], xg[r].reshape(D, SPAN)) * fac[r : r + 1, :]
        cosine, sine = cosT[...], sinT[...]

        def rotated(value):
            a, b = value[0:64], value[64:128]
            return jnp.concatenate([a * cosine - b * sine, b * cosine + a * sine], axis=0)

        qbuf[r, 0:128, :] = rotated(qkv[0:128]).T.astype(BF16)
        qbuf[r, 128:256, :] = rotated(qkv[128:256]).T.astype(BF16)
        kvg[r, 0, 0, 0, 0:128, :] = rotated(qkv[256:384]).astype(BF16)
        kvg[r, 0, 0, 0, 128:256, :] = qkv[384:512].astype(BF16)

    def kv_core(r, dy):
        send(("kvc", r, dy), kvg.at[r, 0, dy], kvg.at[r, 1, dy], to_core)

    def kv_y(name, r, dz):
        send((name, r, 0), kvg.at[r, 0, 0, dz], kvg.at[r, 0, 3, dz], at_y(1))
        send((name, r, 1), kvg.at[r, 0, 0, dz], kvg.at[r, 0, 1, dz], at_y(3))

    def kv_on(name, r, dz):
        send((name, r, 0), kvg.at[r, 0, 3, dz, 0:128], kvg.at[r, 0, 2, dz, 0:128], at_y(1))
        send((name, r, 1), kvg.at[r, 0, 1, dz, 128:256], kvg.at[r, 0, 2, dz, 128:256], at_y(3))

    def kva(r):
        send(("kvz", r), kvg.at[r, 0, 0, 0], kvg.at[r, 0, 0, 1], to_zlo)
        kv_y("kvy1", r, 0)

    def kvb(r):
        recv(("kvz", r))
        kv_y("kvy2", r, 1)
        kv_core(r, 0)

    def kvc(r):
        recv(("kvy1", r, 0))
        recv(("kvy1", r, 1))
        kv_on("kvy3", r, 0)

    def kvd(r):
        recv(("kvy2", r, 0))
        recv(("kvy2", r, 1))
        kv_on("kvy4", r, 1)
        kv_core(r, 1)
        kv_core(r, 3)

    def kve(r):
        for name in ("kvy3", "kvy4"):
            recv((name, r, 0))
            recv((name, r, 1))
        kv_core(r, 2)

    def key_start(b):
        dc, dy, dz = b // 8, (b // 2) % 4, b % 2
        section = ((zlo + dz) % 2) * 2 + (core + dc) % 2
        return (section * 4 + (y + dy) % 4) * SPAN

    def weigh(scores, keep):
        return jnp.where(keep, jnp.exp2(jnp.tanh(scores * (SCALE / CAP)) * (CAP * math.log2(math.e))), 0.0)

    def attend(r):
        for dy in range(4):
            recv(("kvc", r, dy))
        queries = qbuf[r]
        length = lengths[r]
        token = (s * 4 + y) * SPAN + lax.broadcasted_iota(jnp.int32, (256, 128), 0) % SPAN
        limit = jnp.minimum(token, length - 1)
        lane = lax.broadcasted_iota(jnp.int32, (256, 128), 1)

        num = jnp.zeros((256, 128), F32)
        den = jnp.zeros((256, 128), F32)
        for i in range(16):
            keys = kvg.at[r, i // 8, (i // 2) % 4, i % 2]
            weight = weigh(dot(queries, keys[0:128, :]), lane + key_start(i) <= limit)
            num = num + dot_t(weight.astype(BF16), keys[128:256, :])
            den = den + weight
        result = num / jnp.sum(den, axis=-1, keepdims=True)
        for k in range(2):
            attg[r, 0, k] = result[k * 128 : k * 128 + 128].astype(BF16)
        send(("ax1", r, 0), attg.at[r, 0], attg.at[r, 3], at_x(1))
        send(("ax1", r, 1), attg.at[r, 0], attg.at[r, 1], at_x(3))

    def ax2(r):
        recv(("ax1", r, 0))
        recv(("ax1", r, 1))
        send(("ax2", r, 0), attg.at[r, 3, 0], attg.at[r, 2, 0], at_x(1))
        send(("ax2", r, 1), attg.at[r, 1, 1], attg.at[r, 2, 1], at_x(3))

    low, high = pl.ds(0, HALF), pl.ds(HALF, HALF)

    def proj(r):
        recv(("ax2", r, 0))
        recv(("ax2", r, 1))
        attended = [jnp.concatenate([attg[r, d, 0], attg[r, d, 1]], axis=1) for d in range(4)]
        for dz in (2, 1, 3, 0):
            rows = pl.ds(dz * WIDTH, WIDTH)
            part = dot_t(owt[0, rows, :], attended[0])
            for d in range(1, 4):
                part = part + dot_t(owt[d, rows, :], attended[d])
            if dz:
                pb[r, dz] = part.astype(BF16)
            else:
                own[r] = part
            if dz == 2:
                send(("rs1", r, 0), pb.at[r, 2, low], rs1.at[r, 0], at_z(1))
                send(("rs1", r, 1), pb.at[r, 2, high], rs1.at[r, 1], at_z(3))
            if dz == 1:
                send(("rs2", r, 0), pb.at[r, 1, high], rs2.at[r, 0, high], at_z(1))
            if dz == 3:
                send(("rs2", r, 1), pb.at[r, 3, low], rs2.at[r, 1, low], at_z(3))

    def rs_2(r):
        recv(("rs1", r, 0))
        pb[r, 1, 0:HALF] = (pb[r, 1, 0:HALF].astype(F32) + rs1[r, 0].astype(F32)).astype(BF16)
        send(("rs3", r, 0), pb.at[r, 1, low], rs2.at[r, 0, low], at_z(1))
        recv(("rs1", r, 1))
        pb[r, 3, HALF:WIDTH] = (pb[r, 3, HALF:WIDTH].astype(F32) + rs1[r, 1].astype(F32)).astype(BF16)
        send(("rs3", r, 1), pb.at[r, 3, high], rs2.at[r, 1, high], at_z(3))

    def rs_3(r):
        for name in ("rs2", "rs3"):
            recv((name, r, 0))
            recv((name, r, 1))
        share = own[r] + rs2[r, 0].astype(F32) + rs2[r, 1].astype(F32)
        own[r] = share
        ssx[0, r : r + 1, :] = jnp.sum(share * share, axis=0, keepdims=True)

    def c_x():
        for d in (1, 3, 2):
            send(("cx", d), cg.at[0, 0], cg.at[0, 4 - d], at_x(d))

    def c_z():
        for d in (1, 3, 2):
            recv(("cx", d))
        for d in (1, 3, 2):
            send(("cz", d), cg.at[0], cg.at[4 - d], at_z(d))

    lane8 = lax.broadcasted_iota(jnp.int32, (8, 128), 1)

    def c_project():
        for d in (1, 3, 2):
            recv(("cz", d))

        def step(dz, total):
            for dx in range(4):
                head = ((x + dx) % 4) * 4 + (z + dz) % 4
                row = pl.multiple_of(head * WIDTH, 32)
                total = total + dot(cg[dz, dx, 0:16], wraw[pl.ds(row, 128), :])
                total = total + dot(cg[dz, dx, 16:32], wraw[pl.ds(row + 128, 128), :])
                total = total + dot(cg[dz, dx, 32:48, 0:32], wraw[pl.ds(row + 256, 32), :])
            return total

        qkv = lax.fori_loop(0, 4, step, jnp.zeros((16, 512), F32))[0:8] * fac[8:16, 0:1]
        rest = jnp.zeros((8, 128), F32)
        angles = table[pl.ds(lengths[y], 8), :]
        other = pltpu.roll(angles, 64, 1)
        front = lane8 < 64
        cosine = jnp.where(front, angles, other)
        sine = jnp.where(front, -other, angles)

        def rotated(value):
            return value * cosine + pltpu.roll(value, 64, 1) * sine

        cq[...] = jnp.concatenate([rotated(qkv[:, 0:128]), rotated(qkv[:, 128:256])], axis=0).astype(BF16)
        ckv[0] = jnp.concatenate([rotated(qkv[:, 256:384]), rest], axis=0).astype(BF16)
        ckv[1] = jnp.concatenate([qkv[:, 384:512], rest], axis=0).astype(BF16)

    def c_attend():
        queries = cq[...]
        length = lengths[y]
        lane = lax.broadcasted_iota(jnp.int32, (16, 128), 1)

        num = jnp.zeros((16, 128), F32)
        den = jnp.zeros((16, 128), F32)
        for b in range(16):
            keys = kvg.at[y, b // 8, (b // 2) % 4, b % 2]
            weight = weigh(dot(queries, keys[0:128, :]), lane + key_start(b) < length)
            num = num + dot_t(weight.astype(BF16), keys[128:256, :])
            den = den + weight
        near = lax.broadcasted_iota(jnp.int32, (16, 16), 1) <= lax.broadcasted_iota(jnp.int32, (16, 16), 0) % 8
        weight = weigh(dot_t(queries, ckv[0]), near)
        num = num + dot(weight.astype(BF16), ckv[1])
        total = jnp.sum(den, axis=-1, keepdims=True) + jnp.sum(weight, axis=-1, keepdims=True)
        result = num / total
        rest = jnp.zeros((8, 128), F32)
        cattg[0, :, 0:128] = jnp.concatenate([result[0:8], rest], axis=0).astype(BF16)
        cattg[0, :, 128:256] = jnp.concatenate([result[8:16], rest], axis=0).astype(BF16)
        for d in (1, 3, 2):
            send(("ca", d), cattg.at[0], cattg.at[4 - d], at_x(d))

    def c_proj():
        for d in (1, 3, 2):
            recv(("ca", d))
        part = dot_t(cattg[0], owt[0])
        for d in range(1, 4):
            part = part + dot_t(cattg[d], owt[d])
        inside = lax.broadcasted_iota(jnp.int32, (16, 384), 1) < WIDTH
        for dz in range(4):
            moved = part if dz == 0 else pltpu.roll(part, SLAB - dz * WIDTH, 1)
            moved = jnp.where(inside, moved[:, 0:384], 0.0)
            if dz:
                cpj[dz] = moved.astype(BF16)
                send(("cr", dz), cpj.at[dz], crs.at[4 - dz], at_z(dz))
            else:
                cown[...] = moved

    def c_sum():
        share = cown[...]
        for d in (1, 3, 2):
            recv(("cr", d))
        for d in range(1, 4):
            share = share + crs[d].astype(F32)
        cown[...] = share
        ssx[0, 8:24, :] = jnp.broadcast_to(jnp.sum(share * share, axis=-1, keepdims=True), (16, 128))

    def sum_x():
        for d in (1, 3, 2):
            send(("sx", d), ssx.at[0], ssx.at[4 - d], at_x(d))

    def sum_z():
        for d in (1, 3, 2):
            recv(("sx", d))
        ssz[0] = (ssx[0] + ssx[1]) + (ssx[2] + ssx[3])
        for d in (1, 3, 2):
            send(("sz", d), ssz.at[0], ssz.at[4 - d], at_z(d))

    def finish():
        for d in (1, 3, 2):
            recv(("sz", d))
        factor = lax.rsqrt(((ssz[0] + ssz[1]) + (ssz[2] + ssz[3])) / D + EPS)
        for r in range(ROWS):
            part = own[r] * factor[r : r + 1, :] * pgb[...]
            out[r] = (hidden[r].astype(F32) + part).astype(BF16)
        for k in range(3):
            lo, hi = k * 128, min(k * 128 + 128, WIDTH)
            part = cown[0:4, k * 128 : k * 128 + 128] * factor[8:12, :] * gains[1:2, k * 128 : k * 128 + 128]
            c_out[0, :, lo:hi] = (critique[0, :, lo:hi].astype(F32) + part[:, 0 : hi - lo]).astype(BF16)

    x1a(1)
    z1(0)
    x1a(0)
    c_x()
    ow_x()
    fetch_weights()
    turn_weights(0, 6)
    pre_x()
    turn_weights(6, 12)
    turn_weights(12, 18)
    z1(1)
    rope_tables()
    gain_tables()
    e1(0)
    c_z()
    z1(2)
    e1(1)
    z1(3)
    e2(0)
    ow_y1()
    x1a(2)
    pre_z()
    ow_y2()
    e3(0)
    e1(2)
    e2(1)
    x1a(3)
    ow_core()
    e4(0)
    e1(3)
    pre_done()
    project(0)
    c_project()
    kva(0)
    e3(1)
    e2(2)
    e2(3)
    ow_turn()
    kvc(0)
    kvb(0)
    kvd(0)
    e4(1)
    project(1)
    kve(0)
    kva(1)
    e3(2)
    attend(0)
    kvc(1)
    e3(3)
    kvb(1)
    e4(2)
    project(2)
    kva(2)
    ax2(0)
    kvd(1)
    kvc(2)
    kvb(2)
    e4(3)
    project(3)
    kva(3)
    kve(1)
    proj(0)
    kvd(2)
    attend(1)
    kvc(3)
    kvb(3)
    kve(2)
    rs_2(0)
    ax2(1)
    attend(2)
    kvd(3)
    rs_3(0)
    proj(1)
    kve(3)
    ax2(2)
    attend(3)
    rs_2(1)
    c_attend()
    proj(2)
    ax2(3)
    c_proj()
    rs_3(1)
    proj(3)
    rs_2(2)
    c_sum()
    rs_2(3)
    rs_3(2)
    rs_3(3)
    sum_x()
    sum_z()
    finish()
    for copy in copies.values():
        copy.wait_send()


def hand_over(result, c_result, out, c_out):
    out[...] = result[...]
    c_out[...] = c_result[...]


def body(hidden, critique, lengths, pre_gain, post_gain, q_weight, k_weight, v_weight, o_weight):
    table = jnp.asarray(rope_table())
    vmem = pl.BlockSpec(memory_space=pltpu.VMEM)
    smem = pl.BlockSpec(memory_space=pltpu.SMEM)
    anywhere = pl.BlockSpec(memory_space=pl.ANY)
    turned = jnp.transpose(hidden, (0, 2, 1))
    result, c_result = pl.pallas_call(
        kernel,
        out_shape=(
            jax.ShapeDtypeStruct(turned.shape, BF16),
            jax.ShapeDtypeStruct(critique.shape, BF16),
        ),
        in_specs=[vmem, vmem, smem, vmem, vmem, anywhere, anywhere, anywhere, anywhere, anywhere],
        out_specs=(vmem, vmem),
        scratch_shapes=[
            pltpu.VMEM((ROWS, 4, 4, WIDTH, SPAN), BF16),
            pltpu.VMEM((D, 512), BF16),
            pltpu.VMEM((512, D), BF16),
            pltpu.VMEM((WIDTH, 128), F32),
            pltpu.VMEM((2056, 128), F32),
            pltpu.VMEM((64, SPAN), F32),
            pltpu.VMEM((64, SPAN), F32),
            pltpu.VMEM((ROWS, 256, HEAD), BF16),
            pltpu.VMEM((ROWS, 2, 4, 2, 256, SPAN), BF16),
            pltpu.VMEM((ROWS, 4, 2, SPAN, HEAD), BF16),
            pltpu.VMEM((4, 256, SLAB), BF16),
            pltpu.VMEM((4, SLAB, 256), BF16),
            pltpu.VMEM((ROWS, 4, WIDTH, SPAN), BF16),
            pltpu.VMEM((ROWS, WIDTH, SPAN), F32),
            pltpu.VMEM((ROWS, 2, HALF, SPAN), BF16),
            pltpu.VMEM((ROWS, 2, WIDTH, SPAN), BF16),
            pltpu.VMEM((4, 4, 48, 128), BF16),
            pltpu.VMEM((16, 128), BF16),
            pltpu.VMEM((2, 16, 128), BF16),
            pltpu.VMEM((4, 16, 256), BF16),
            pltpu.VMEM((4, 16, 384), BF16),
            pltpu.VMEM((16, 384), F32),
            pltpu.VMEM((4, 16, 384), BF16),
            pltpu.VMEM((4, 24, 128), F32),
            pltpu.VMEM((4, 24, 128), F32),
            pltpu.VMEM((4, 16, 128), F32),
            pltpu.VMEM((4, 16, 128), F32),
            pltpu.VMEM((16, 128), F32),
            pltpu.VMEM((8, 384), F32),
            pltpu.SemaphoreType.DMA((N_SEM,)),
            pltpu.SemaphoreType.DMA((N_SEM,)),
            pltpu.SemaphoreType.DMA((8,)),
        ],
        compiler_params=pltpu.CompilerParams(
            collective_id=0, has_side_effects=True, vmem_limit_bytes=56 * 1024 * 1024
        ),
        cost_estimate=pl.CostEstimate(flops=5_000_000_000, bytes_accessed=16_000_000, transcendentals=4_000_000),
    )(turned, critique, lengths, pre_gain.reshape(16, WIDTH), post_gain.reshape(1, WIDTH), table, q_weight, k_weight, v_weight, o_weight)
    result, c_result = pl.pallas_call(
        hand_over,
        out_shape=(
            jax.ShapeDtypeStruct(turned.shape, BF16),
            jax.ShapeDtypeStruct(critique.shape, BF16),
        ),
        in_specs=[vmem, vmem],
        out_specs=(vmem, vmem),
    )(result, c_result)
    return jnp.transpose(result, (0, 2, 1)), c_result


def solution(mesh):
    return jax.shard_map(
        body,
        mesh=mesh,
        in_specs=(
            P(None, ("section", "seq"), "head"),
            P("seq", None, "head"),
            P(),
            P(),
            P("head"),
            P(None, "head"),
            P(None, "head"),
            P(None, "head"),
            P("head", None),
        ),
        out_specs=(P(None, ("section", "seq"), "head"), P("seq", None, "head")),
        check_vma=False,
    )
```

```python
import math

import jax
import jax.numpy as jnp
import numpy as np
from jax import lax
from jax.experimental import pallas as pl
from jax.experimental.pallas import tpu as pltpu
from jax.sharding import PartitionSpec as P

D = 4608
HEADS = 32
KV_HEADS = 16
HEAD = 128
ROWS = 4
SPAN = 128
WIDTH = 288
SLAB = 4 * WIDTH
HALF = WIDTH // 2
STEPS = 4

EPS = 1e-06
CAP = 50.0
BASE = 10000.0
SCALE = (D // HEADS) ** (-0.5)
F32 = jnp.float32
BF16 = jnp.bfloat16
MESH = pl.DeviceIdType.MESH
N_SEM = 184


def rope_table():
    freq = np.exp(np.arange(64, dtype=np.float64) * (-2.0 * math.log(BASE) / HEAD))
    angle = np.arange(2056, dtype=np.float64)[:, None] * freq
    return np.concatenate([np.cos(angle), np.sin(angle)], axis=-1).astype(np.float32)


def dot(a, b):
    return jnp.dot(a, b, preferred_element_type=F32)


def dot_t(a, b):
    return lax.dot_general(a, b, (((1,), (1,)), ((), ())), preferred_element_type=F32)


def kernel(
    hidden, critique, lengths, gains, table_hbm, wq, wk, wv, wo,
    out, c_out,
    xg, wraw, wt, pgb, table, cosT, sinT, qbuf, kvg, attg, owslab, owt,
    pb, own, rs1, rs2, cg, cq, ckv, cattg, cpj, cown, crs, ssx, ssz, prex, prez, fac,
    send_sem, recv_sem, local_sem,
):
    s = lax.axis_index("section")
    y = lax.axis_index("seq")
    h = lax.axis_index("head")
    x, z = h // 4, h % 4
    zlo, core = s // 2, s % 2

    def at_x(d):
        return {"head": ((x + d) % 4) * 4 + z}

    def at_z(d):
        return {"head": x * 4 + (z + d) % 4}

    def at_y(d):
        return {"seq": (y + d) % 4}

    to_zlo = {"section": (1 - zlo) * 2 + core}
    to_core = {"section": zlo * 2 + 1 - core}

    partners = [at_x(1), at_x(3), at_x(2), at_z(1), at_z(3), at_z(2), at_y(1), at_y(3), to_zlo, to_core]
    barrier = pltpu.get_barrier_semaphore()
    for partner in partners:
        pl.semaphore_signal(barrier, inc=1, device_id=partner, device_id_type=MESH)

    copies = {}

    def send(name, src, dst, device):
        i = len(copies)
        assert i < N_SEM
        copy = pltpu.make_async_remote_copy(
            src_ref=src, dst_ref=dst, send_sem=send_sem.at[i], recv_sem=recv_sem.at[i],
            device_id=device, device_id_type=MESH,
        )
        copy.start()
        copies[name] = copy

    def recv(name):
        copies[name].wait_recv()

    local = []

    def fetch(src, dst):
        copy = pltpu.make_async_copy(src, dst, local_sem.at[len(local)])
        copy.start()
        local.append(copy)
        return copy

    piece = pl.multiple_of(core * 128 + y * 32, 32)
    own_cols = pl.ds(pl.multiple_of(x * SLAB, 128), SLAB)
    fetch_w = [
        fetch(wq, wraw.at[:, 0:256]),
        fetch(wk, wraw.at[:, 256:384]),
        fetch(wv, wraw.at[:, 384:512]),
    ]
    fetch_table = fetch(table_hbm, table)
    fetch_o = fetch(wo.at[pl.ds(piece, 32), own_cols], owslab.at[0, pl.ds(piece, 32), :])

    def column(row, k):
        n = 128 if k < 2 else 32
        return jnp.broadcast_to(gains[:, k * 128 : k * 128 + 128].T[0:n, row : row + 1], (n, 128))

    gain = jnp.concatenate([column(0, k) for k in range(3)], axis=0)
    for r in range(ROWS):
        block = hidden[r].astype(F32)
        xg[r, x, z] = (block * gain).astype(BF16)
        prex[0, r : r + 1, :] = jnp.sum(block * block, axis=0, keepdims=True)
    c_rows = jnp.concatenate([critique[0].astype(F32), jnp.zeros((12, WIDTH), F32)], axis=0)
    c_sums = jnp.sum(c_rows * c_rows, axis=-1, keepdims=True)
    prex[0, 4:8, :] = jnp.zeros((4, 128), F32)
    prex[0, 8:16, :] = jnp.broadcast_to(c_sums[0:8], (8, 128))
    c_rows = c_rows * gains[0:1, 0:WIDTH]
    c_last = jnp.concatenate([c_rows[:, 256:288], jnp.zeros((16, 96), F32)], axis=1)
    cg[0, 0] = jnp.concatenate([c_rows[:, 0:128], c_rows[:, 128:256], c_last], axis=0).astype(BF16)

    ssx[0] = jnp.zeros((24, 128), F32)
    pl.semaphore_wait(barrier, len(partners))

    zr, zl, zo = (z + 1) % 4, (z + 3) % 4, (z + 2) % 4
    xr, xl, xo = (x + 1) % 4, (x + 3) % 4, (x + 2) % 4
    main = pl.ds(0, WIDTH)
    main_up, main_down = pl.ds(0, HALF), pl.ds(HALF, HALF)

    def pair_send(name, up, down, where):
        send(name + (0,), up, up, where(1))
        send(name + (1,), down, down, where(3))

    def z1(r):
        block = xg.at[r, x, z, main]
        pair_send(("z1", r), block, block, at_z)

    def x1(r, k, place):
        block = xg.at[r, x, place, main]
        pair_send(("x1", r, k), block, block, at_x)

    def x1a(r):
        x1(r, 0, z)

    def e1(r):
        recv(("z1", r, 0))
        recv(("z1", r, 1))
        pair_send(("z2", r), xg.at[r, x, zl, main_up], xg.at[r, x, zr, main_down], at_z)
        x1(r, 1, zl)
        x1(r, 3, zr)

    def e2(r):
        recv(("z2", r, 0))
        recv(("z2", r, 1))
        x1(r, 2, zo)

    def e3(r):
        for k in range(4):
            recv(("x1", r, k, 0))
            recv(("x1", r, k, 1))
        pair_send(("x2", r), xg.at[r, xl, :, main_up], xg.at[r, xr, :, main_down], at_x)

    def e4(r):
        recv(("x2", r, 0))
        recv(("x2", r, 1))

    def ow_x():
        for d in (1, 3, 2):
            cols = pl.ds(pl.multiple_of(((x + d) % 4) * SLAB, 128), SLAB)
            send(("ow", d), wo.at[pl.ds(piece, 32), cols], owslab.at[4 - d, pl.ds(piece, 32), :], at_x(d))

    def ow_y1():
        fetch_o.wait()
        for d in (1, 3, 2):
            recv(("ow", d))
        here = owslab.at[:, pl.ds(piece, 32), :]
        send("owy1r", here, here, at_y(1))
        send("owy1l", here, here, at_y(3))

    def ow_y2():
        low = pl.ds(pl.multiple_of(core * 128 + ((y + 3) % 4) * 32, 32), 16)
        high = pl.ds(pl.multiple_of(core * 128 + ((y + 1) % 4) * 32 + 16, 16), 16)
        recv("owy1r")
        send("owy2r", owslab.at[:, low, :], owslab.at[:, low, :], at_y(1))
        recv("owy1l")
        send("owy2l", owslab.at[:, high, :], owslab.at[:, high, :], at_y(3))

    def ow_core():
        recv("owy2r")
        recv("owy2l")
        half = owslab.at[:, pl.ds(pl.multiple_of(core * 128, 128), 128), :]
        send("owc", half, half, to_core)

    def ow_turn():
        recv("owc")

        def step(d, carry):
            turned = owslab[d].T
            for zz in range(4):
                row = pl.multiple_of(((zz - z + 4) % 4) * WIDTH, 32)
                owt[d, pl.ds(row, WIDTH), :] = turned[zz * WIDTH : (zz + 1) * WIDTH]
            return carry

        lax.fori_loop(0, 4, step, 0)

    def gain_tables():
        for k in range(3):
            pgb[k * 128 : min(k * 128 + 128, WIDTH), :] = column(1, k)

    def rope_tables():
        fetch_table.wait()
        place = pl.multiple_of((s * 4 + y) * SPAN, SPAN)
        turned = table[pl.ds(place, SPAN), :].T
        cosT[...] = turned[0:64]
        sinT[...] = turned[64:128]

    def fetch_weights():
        for copy in fetch_w:
            copy.wait()

    def turn_weights(lo, hi):
        def step(c, carry):
            row = pl.multiple_of(c * 256, 256)
            wt[:, pl.ds(row, 256)] = wraw[pl.ds(row, 256), :].T
            return carry

        lax.fori_loop(lo, hi, step, 0)

    def pre_x():
        for d in (1, 3, 2):
            send(("px", d), prex.at[0], prex.at[4 - d], at_x(d))

    def pre_z():
        for d in (1, 3, 2):
            recv(("px", d))
        prez[0] = (prex[0] + prex[1]) + (prex[2] + prex[3])
        for d in (1, 3, 2):
            send(("pz", d), prez.at[0], prez.at[4 - d], at_z(d))

    def pre_done():
        for d in (1, 3, 2):
            recv(("pz", d))
        fac[...] = lax.rsqrt(((prez[0] + prez[1]) + (prez[2] + prez[3])) / D + EPS)

    def project(r):
        qkv = dot(wt[...], xg[r].reshape(D, SPAN)) * fac[r : r + 1, :]
        cosine, sine = cosT[...], sinT[...]

        def rotated(value):
            a, b = value[0:64], value[64:128]
            return jnp.concatenate([a * cosine - b * sine, b * cosine + a * sine], axis=0)

        qbuf[r, 0:128, :] = rotated(qkv[0:128]).T.astype(BF16)
        qbuf[r, 128:256, :] = rotated(qkv[128:256]).T.astype(BF16)
        kvg[r, 0, 0, 0, 0:128, :] = rotated(qkv[256:384]).astype(BF16)
        kvg[r, 0, 0, 0, 128:256, :] = qkv[384:512].astype(BF16)

    def kv_core(r, dy):
        send(("kvc", r, dy), kvg.at[r, 0, dy], kvg.at[r, 1, dy], to_core)

    def kv_y(name, r, dz):
        send((name, r, 0), kvg.at[r, 0, 0, dz], kvg.at[r, 0, 3, dz], at_y(1))
        send((name, r, 1), kvg.at[r, 0, 0, dz], kvg.at[r, 0, 1, dz], at_y(3))

    def kv_on(name, r, dz):
        send((name, r, 0), kvg.at[r, 0, 3, dz, 0:128], kvg.at[r, 0, 2, dz, 0:128], at_y(1))
        send((name, r, 1), kvg.at[r, 0, 1, dz, 128:256], kvg.at[r, 0, 2, dz, 128:256], at_y(3))

    def kva(r):
        send(("kvz", r), kvg.at[r, 0, 0, 0], kvg.at[r, 0, 0, 1], to_zlo)
        kv_y("kvy1", r, 0)

    def kvb(r):
        recv(("kvz", r))
        kv_y("kvy2", r, 1)
        kv_core(r, 0)

    def kvc(r):
        recv(("kvy1", r, 0))
        recv(("kvy1", r, 1))
        kv_on("kvy3", r, 0)

    def kvd(r):
        recv(("kvy2", r, 0))
        recv(("kvy2", r, 1))
        kv_on("kvy4", r, 1)
        kv_core(r, 1)
        kv_core(r, 3)

    def kve(r):
        for name in ("kvy3", "kvy4"):
            recv((name, r, 0))
            recv((name, r, 1))
        kv_core(r, 2)

    def key_start(b):
        dc, dy, dz = b // 8, (b // 2) % 4, b % 2
        section = ((zlo + dz) % 2) * 2 + (core + dc) % 2
        return (section * 4 + (y + dy) % 4) * SPAN

    def weigh(scores, keep):
        return jnp.where(keep, jnp.exp2(jnp.tanh(scores * (SCALE / CAP)) * (CAP * math.log2(math.e))), 0.0)

    def attend(r):
        for dy in range(4):
            recv(("kvc", r, dy))
        queries = qbuf[r]
        length = lengths[r]
        token = (s * 4 + y) * SPAN + lax.broadcasted_iota(jnp.int32, (256, 128), 0) % SPAN
        limit = jnp.minimum(token, length - 1)
        lane = lax.broadcasted_iota(jnp.int32, (256, 128), 1)

        num = jnp.zeros((256, 128), F32)
        den = jnp.zeros((256, 128), F32)
        for i in range(16):
            keys = kvg.at[r, i // 8, (i // 2) % 4, i % 2]
            weight = weigh(dot(queries, keys[0:128, :]), lane + key_start(i) <= limit)
            num = num + dot_t(weight.astype(BF16), keys[128:256, :])
            den = den + weight
        result = num / jnp.sum(den, axis=-1, keepdims=True)
        for k in range(2):
            attg[r, 0, k] = result[k * 128 : k * 128 + 128].astype(BF16)
        send(("ax1", r, 0), attg.at[r, 0], attg.at[r, 3], at_x(1))
        send(("ax1", r, 1), attg.at[r, 0], attg.at[r, 1], at_x(3))

    def ax2(r):
        recv(("ax1", r, 0))
        recv(("ax1", r, 1))
        send(("ax2", r, 0), attg.at[r, 3, 0], attg.at[r, 2, 0], at_x(1))
        send(("ax2", r, 1), attg.at[r, 1, 1], attg.at[r, 2, 1], at_x(3))

    low, high = pl.ds(0, HALF), pl.ds(HALF, HALF)

    def proj(r):
        recv(("ax2", r, 0))
        recv(("ax2", r, 1))
        attended = [jnp.concatenate([attg[r, d, 0], attg[r, d, 1]], axis=1) for d in range(4)]
        for dz in (2, 1, 3, 0):
            rows = pl.ds(dz * WIDTH, WIDTH)
            part = dot_t(owt[0, rows, :], attended[0])
            for d in range(1, 4):
                part = part + dot_t(owt[d, rows, :], attended[d])
            if dz:
                pb[r, dz] = part.astype(BF16)
            else:
                own[r] = part
            if dz == 2:
                send(("rs1", r, 0), pb.at[r, 2, low], rs1.at[r, 0], at_z(1))
                send(("rs1", r, 1), pb.at[r, 2, high], rs1.at[r, 1], at_z(3))
            if dz == 1:
                send(("rs2", r, 0), pb.at[r, 1, high], rs2.at[r, 0, high], at_z(1))
            if dz == 3:
                send(("rs2", r, 1), pb.at[r, 3, low], rs2.at[r, 1, low], at_z(3))

    def rs_2(r):
        recv(("rs1", r, 0))
        pb[r, 1, 0:HALF] = (pb[r, 1, 0:HALF].astype(F32) + rs1[r, 0].astype(F32)).astype(BF16)
        send(("rs3", r, 0), pb.at[r, 1, low], rs2.at[r, 0, low], at_z(1))
        recv(("rs1", r, 1))
        pb[r, 3, HALF:WIDTH] = (pb[r, 3, HALF:WIDTH].astype(F32) + rs1[r, 1].astype(F32)).astype(BF16)
        send(("rs3", r, 1), pb.at[r, 3, high], rs2.at[r, 1, high], at_z(3))

    def rs_3(r):
        for name in ("rs2", "rs3"):
            recv((name, r, 0))
            recv((name, r, 1))
        share = own[r] + rs2[r, 0].astype(F32) + rs2[r, 1].astype(F32)
        own[r] = share
        ssx[0, r : r + 1, :] = jnp.sum(share * share, axis=0, keepdims=True)

    def c_x():
        for d in (1, 3, 2):
            send(("cx", d), cg.at[0, 0], cg.at[0, 4 - d], at_x(d))

    def c_z():
        for d in (1, 3, 2):
            recv(("cx", d))
        for d in (1, 3, 2):
            send(("cz", d), cg.at[0], cg.at[4 - d], at_z(d))

    lane8 = lax.broadcasted_iota(jnp.int32, (8, 128), 1)

    def c_project():
        for d in (1, 3, 2):
            recv(("cz", d))

        def step(dz, total):
            for dx in range(4):
                head = ((x + dx) % 4) * 4 + (z + dz) % 4
                row = pl.multiple_of(head * WIDTH, 32)
                total = total + dot(cg[dz, dx, 0:16], wraw[pl.ds(row, 128), :])
                total = total + dot(cg[dz, dx, 16:32], wraw[pl.ds(row + 128, 128), :])
                total = total + dot(cg[dz, dx, 32:48, 0:32], wraw[pl.ds(row + 256, 32), :])
            return total

        qkv = lax.fori_loop(0, 4, step, jnp.zeros((16, 512), F32))[0:8] * fac[8:16, 0:1]
        rest = jnp.zeros((8, 128), F32)
        angles = table[pl.ds(lengths[y], 8), :]
        other = pltpu.roll(angles, 64, 1)
        front = lane8 < 64
        cosine = jnp.where(front, angles, other)
        sine = jnp.where(front, -other, angles)

        def rotated(value):
            return value * cosine + pltpu.roll(value, 64, 1) * sine

        cq[...] = jnp.concatenate([rotated(qkv[:, 0:128]), rotated(qkv[:, 128:256])], axis=0).astype(BF16)
        ckv[0] = jnp.concatenate([rotated(qkv[:, 256:384]), rest], axis=0).astype(BF16)
        ckv[1] = jnp.concatenate([qkv[:, 384:512], rest], axis=0).astype(BF16)

    def c_attend():
        queries = cq[...]
        length = lengths[y]
        lane = lax.broadcasted_iota(jnp.int32, (16, 128), 1)

        num = jnp.zeros((16, 128), F32)
        den = jnp.zeros((16, 128), F32)
        for b in range(16):
            keys = kvg.at[y, b // 8, (b // 2) % 4, b % 2]
            weight = weigh(dot(queries, keys[0:128, :]), lane + key_start(b) < length)
            num = num + dot_t(weight.astype(BF16), keys[128:256, :])
            den = den + weight
        near = lax.broadcasted_iota(jnp.int32, (16, 16), 1) <= lax.broadcasted_iota(jnp.int32, (16, 16), 0) % 8
        weight = weigh(dot_t(queries, ckv[0]), near)
        num = num + dot(weight.astype(BF16), ckv[1])
        total = jnp.sum(den, axis=-1, keepdims=True) + jnp.sum(weight, axis=-1, keepdims=True)
        result = num / total
        rest = jnp.zeros((8, 128), F32)
        cattg[0, :, 0:128] = jnp.concatenate([result[0:8], rest], axis=0).astype(BF16)
        cattg[0, :, 128:256] = jnp.concatenate([result[8:16], rest], axis=0).astype(BF16)
        for d in (1, 3, 2):
            send(("ca", d), cattg.at[0], cattg.at[4 - d], at_x(d))

    def c_proj():
        for d in (1, 3, 2):
            recv(("ca", d))
        part = dot_t(cattg[0], owt[0])
        for d in range(1, 4):
            part = part + dot_t(cattg[d], owt[d])
        inside = lax.broadcasted_iota(jnp.int32, (16, 384), 1) < WIDTH
        for dz in range(4):
            moved = part if dz == 0 else pltpu.roll(part, SLAB - dz * WIDTH, 1)
            moved = jnp.where(inside, moved[:, 0:384], 0.0)
            if dz:
                cpj[dz] = moved.astype(BF16)
                send(("cr", dz), cpj.at[dz], crs.at[4 - dz], at_z(dz))
            else:
                cown[...] = moved

    def c_sum():
        share = cown[...]
        for d in (1, 3, 2):
            recv(("cr", d))
        for d in range(1, 4):
            share = share + crs[d].astype(F32)
        cown[...] = share
        ssx[0, 8:24, :] = jnp.broadcast_to(jnp.sum(share * share, axis=-1, keepdims=True), (16, 128))

    def sum_x():
        for d in (1, 3, 2):
            send(("sx", d), ssx.at[0], ssx.at[4 - d], at_x(d))

    def sum_z():
        for d in (1, 3, 2):
            recv(("sx", d))
        ssz[0] = (ssx[0] + ssx[1]) + (ssx[2] + ssx[3])
        for d in (1, 3, 2):
            send(("sz", d), ssz.at[0], ssz.at[4 - d], at_z(d))

    def finish():
        for d in (1, 3, 2):
            recv(("sz", d))
        factor = lax.rsqrt(((ssz[0] + ssz[1]) + (ssz[2] + ssz[3])) / D + EPS)
        for r in range(ROWS):
            part = own[r] * factor[r : r + 1, :] * pgb[...]
            out[r] = (hidden[r].astype(F32) + part).astype(BF16)
        for k in range(3):
            lo, hi = k * 128, min(k * 128 + 128, WIDTH)
            part = cown[0:4, k * 128 : k * 128 + 128] * factor[8:12, :] * gains[1:2, k * 128 : k * 128 + 128]
            c_out[0, :, lo:hi] = (critique[0, :, lo:hi].astype(F32) + part[:, 0 : hi - lo]).astype(BF16)

    x1a(1)
    fetch_weights()
    x1a(0)
    turn_weights(0, 6)
    pre_x()
    turn_weights(6, 12)
    turn_weights(12, 18)
    ow_x()
    gain_tables()
    z1(0)
    c_x()
    rope_tables()
    z1(1)
    pre_z()
    e1(0)
    z1(2)
    ow_y1()
    c_z()
    e1(1)
    z1(3)
    pre_done()
    e2(0)
    x1a(2)
    e1(2)
    ow_y2()
    e3(0)
    ow_core()
    c_project()
    e2(1)
    x1a(3)
    e4(0)
    project(0)
    kva(0)
    e3(1)
    e1(3)
    e2(2)
    ow_turn()
    kvb(0)
    kvc(0)
    e2(3)
    e4(1)
    project(1)
    kvd(0)
    kva(1)
    kve(0)
    kvb(1)
    e3(2)
    kvc(1)
    attend(0)
    e3(3)
    kvd(1)
    e4(2)
    project(2)
    kve(1)
    kva(2)
    ax2(0)
    attend(1)
    kvc(2)
    kvb(2)
    e4(3)
    project(3)
    kva(3)
    proj(0)
    ax2(1)
    kvd(2)
    proj(1)
    kve(2)
    kvb(3)
    rs_2(0)
    kvc(3)
    attend(2)
    kvd(3)
    rs_2(1)
    kve(3)
    ax2(2)
    rs_3(0)
    attend(3)
    proj(2)
    rs_3(1)
    c_attend()
    ax2(3)
    c_proj()
    rs_2(2)
    proj(3)
    c_sum()
    rs_3(2)
    rs_2(3)
    rs_3(3)
    sum_x()
    sum_z()
    finish()
    for copy in copies.values():
        copy.wait_send()


def hand_over(result, c_result, out, c_out):
    out[...] = result[...]
    c_out[...] = c_result[...]


def body(hidden, critique, lengths, pre_gain, post_gain, q_weight, k_weight, v_weight, o_weight):
    own_gain = lax.dynamic_slice(pre_gain, (lax.axis_index("head") * WIDTH,), (WIDTH,))
    gains = jnp.pad(jnp.stack([own_gain, post_gain]).astype(F32), ((0, 6), (0, 384 - WIDTH)))
    table = jnp.asarray(rope_table())
    vmem = pl.BlockSpec(memory_space=pltpu.VMEM)
    smem = pl.BlockSpec(memory_space=pltpu.SMEM)
    anywhere = pl.BlockSpec(memory_space=pl.ANY)
    turned = jnp.transpose(hidden, (0, 2, 1))
    result, c_result = pl.pallas_call(
        kernel,
        out_shape=(
            jax.ShapeDtypeStruct(turned.shape, BF16),
            jax.ShapeDtypeStruct(critique.shape, BF16),
        ),
        in_specs=[vmem, vmem, smem, vmem, anywhere, anywhere, anywhere, anywhere, anywhere],
        out_specs=(vmem, vmem),
        scratch_shapes=[
            pltpu.VMEM((ROWS, 4, 4, WIDTH, SPAN), BF16),
            pltpu.VMEM((D, 512), BF16),
            pltpu.VMEM((512, D), BF16),
            pltpu.VMEM((WIDTH, 128), F32),
            pltpu.VMEM((2056, 128), F32),
            pltpu.VMEM((64, SPAN), F32),
            pltpu.VMEM((64, SPAN), F32),
            pltpu.VMEM((ROWS, 256, HEAD), BF16),
            pltpu.VMEM((ROWS, 2, 4, 2, 256, SPAN), BF16),
            pltpu.VMEM((ROWS, 4, 2, SPAN, HEAD), BF16),
            pltpu.VMEM((4, 256, SLAB), BF16),
            pltpu.VMEM((4, SLAB, 256), BF16),
            pltpu.VMEM((ROWS, 4, WIDTH, SPAN), BF16),
            pltpu.VMEM((ROWS, WIDTH, SPAN), F32),
            pltpu.VMEM((ROWS, 2, HALF, SPAN), BF16),
            pltpu.VMEM((ROWS, 2, WIDTH, SPAN), BF16),
            pltpu.VMEM((4, 4, 48, 128), BF16),
            pltpu.VMEM((16, 128), BF16),
            pltpu.VMEM((2, 16, 128), BF16),
            pltpu.VMEM((4, 16, 256), BF16),
            pltpu.VMEM((4, 16, 384), BF16),
            pltpu.VMEM((16, 384), F32),
            pltpu.VMEM((4, 16, 384), BF16),
            pltpu.VMEM((4, 24, 128), F32),
            pltpu.VMEM((4, 24, 128), F32),
            pltpu.VMEM((4, 16, 128), F32),
            pltpu.VMEM((4, 16, 128), F32),
            pltpu.VMEM((16, 128), F32),
            pltpu.SemaphoreType.DMA((N_SEM,)),
            pltpu.SemaphoreType.DMA((N_SEM,)),
            pltpu.SemaphoreType.DMA((8,)),
        ],
        compiler_params=pltpu.CompilerParams(
            collective_id=0, has_side_effects=True, vmem_limit_bytes=56 * 1024 * 1024
        ),
        cost_estimate=pl.CostEstimate(flops=5_000_000_000, bytes_accessed=16_000_000, transcendentals=4_000_000),
    )(turned, critique, lengths, gains, table, q_weight, k_weight, v_weight, o_weight)
    result, c_result = pl.pallas_call(
        hand_over,
        out_shape=(
            jax.ShapeDtypeStruct(turned.shape, BF16),
            jax.ShapeDtypeStruct(critique.shape, BF16),
        ),
        in_specs=[vmem, vmem],
        out_specs=(vmem, vmem),
    )(result, c_result)
    return jnp.transpose(result, (0, 2, 1)), c_result


def solution(mesh):
    return jax.shard_map(
        body,
        mesh=mesh,
        in_specs=(
            P(None, ("section", "seq"), "head"),
            P("seq", None, "head"),
            P(),
            P(),
            P("head"),
            P(None, "head"),
            P(None, "head"),
            P(None, "head"),
            P("head", None),
        ),
        out_specs=(P(None, ("section", "seq"), "head"), P("seq", None, "head")),
        check_vma=False,
    )
```
